128 devices in a mesh: owner: 16 (over z, x), worker: 8 (over y, core).
Axes of the slice: x: 4, y: 4, z: 4, core: 2. Of those that a mesh axis runs over, the one named last changes fastest.
Arguments:
- embeddings: bfloat16 [262144, 4096], P(('owner', 'worker')), may hold values from -6 to 6
- row_cluster: int32 [262144], P(('owner', 'worker')), may hold values from 0 to 63
- block_owner: int32 [2048], P(('owner', 'worker')), may hold values from 0 to 15, as said below
- routing: int32 [16, 8, 16], replicated, may hold values from 0 to 7, as said below
Outputs:
- row_best: float32 [262144], P(('owner', 'worker'))
The draws below stay inside these ranges and needn't reach their ends.
Inputs may be any that keep to these rules, and one draw needn't show every extreme that they name: `block_owner`: the 16 blocks of one device go to 16 different owner indices, each owner index once. routing[p, w, o] is the worker index to which device (p, w) passes on the block that device (o, w) sends to owner p. For fixed p and o the 8 values over w all differ; for fixed p and w (over o), and for fixed o and w (over p), every worker index is named exactly 2 times.
All inputs are finite; a program needn't handle non-finite values.
Results may differ from the reference program's by a relative error of at most 0.0003.
Values may be sent and summed in bfloat16 or wider, within the bound.
A program may use at most 128 MiB of HBM per device.

```python
import math
import jax
import jax.numpy as jnp
import numpy as np
from jax import lax

D = 4096
BLK = 128
LABELS = 64
NB = 16
ROWS = 262144
N_OWNER = 16
N_WORKER = 8


def shuffle_owners(item_key):
    return jax.random.permutation(item_key, N_OWNER).astype(jnp.int32)


def plan_tables(seed_key):
    key_send, key_first, key_second, key_order = jax.random.split(seed_key, 4)
    owners = jax.vmap(shuffle_owners)(jax.random.split(key_send, N_OWNER * N_WORKER)).reshape(-1)
    source_shift = jax.random.permutation(key_first, N_OWNER).astype(jnp.int32) % N_WORKER
    target_shift = jax.random.permutation(key_second, N_OWNER).astype(jnp.int32) % N_WORKER
    relabel = jax.random.permutation(key_order, N_WORKER).astype(jnp.int32)
    worker_iota = jnp.arange(N_WORKER, dtype=jnp.int32)
    position = (worker_iota[None, :, None] + source_shift[None, None, :] + target_shift[:, None, None]) % N_WORKER
    routing = relabel[position]
    return (owners.astype(jnp.int32), routing.astype(jnp.int32))


def draw_block_owner(key, part):
    owners, routing = plan_tables(key)
    return owners


def draw_routing(key, part):
    owners, routing = plan_tables(key)
    return routing


def place_ends(drawn, own_key, least, high):
    longest = drawn.shape.index(max(drawn.shape))
    spots = []
    for shift in (0, 1):
        where = [jax.random.randint(jax.random.fold_in(own_key, axis), (), 0, length) for axis, length in enumerate(drawn.shape)]
        where[longest] = (where[longest] + shift) % drawn.shape[longest]
        spots.append(tuple(where))
    return drawn.at[spots[0]].set(least).at[spots[1]].set(high)


def level_of(stream_key, extent, pieces, smallest, largest):
    loudness = 1.0
    for dim, blocks in pieces:
        draws = jax.random.uniform(jax.random.fold_in(jax.random.fold_in(stream_key, 6), dim), (blocks,), jnp.float32, smallest / len(pieces), largest / len(pieces))
        loudness = loudness * jnp.repeat(jnp.exp(draws), extent[dim] // blocks).reshape((-1,) + (1,) * (len(extent) - 1 - dim))
    return loudness


def rank_table(amount, skew):
    weights = [(1 << 20) // math.isqrt(rank ** skew) + 1 for rank in range(1, amount + 1)]
    width = 1 + sum(weights) // (1 << 30)
    return np.cumsum(np.array([max(1, weight // width) for weight in weights]))


def ranked(own_key, dims, count, lean):
    table = rank_table(count, lean)
    ticket = jax.random.randint(jax.random.fold_in(own_key, 1), dims, 0, int(table[count - 1]))
    rank = jnp.searchsorted(jnp.asarray(table, jnp.int32), ticket, side="right")
    return jax.random.permutation(jax.random.fold_in(own_key, 2), count)[rank].astype(jnp.int32)


def normal_values(stream_key, shape, scale, most, shards=(), kind=jnp.bfloat16):
    array = jax.random.normal(stream_key, shape, jnp.float32) * scale
    if len(shards) > 0:
        array = level_of(stream_key, shape, shards, -0.22, 0.18) * array
    return jnp.clip(array, min=-most, max=most).astype(kind)


def setup_inputs(seed: int = 0) -> dict:
    streams_of = jax.random.split(jax.random.key(seed), 5)
    embeddings = normal_values(streams_of[0], (ROWS, D), 1.0, 6.0, ((0, 128),))
    row_cluster = place_ends(ranked(streams_of[1], (ROWS,), LABELS, 2), jax.random.fold_in(streams_of[1], 3), 0, LABELS - 1).astype(jnp.int32)
    block_owner = draw_block_owner(jax.random.fold_in(streams_of[4], 71), 0)
    routing = draw_routing(jax.random.fold_in(streams_of[4], 71), 0)
    return {"embeddings": embeddings, "row_cluster": row_cluster, "block_owner": block_owner, "routing": routing}


def reference(embeddings, row_cluster, block_owner, routing):
    block_total = N_OWNER * N_WORKER * NB
    member_rows = N_OWNER * BLK
    blocks = embeddings.reshape(block_total, BLK, D)
    labels = row_cluster.reshape(block_total, BLK)
    scales = lax.rsqrt(lax.optimization_barrier(jnp.mean(jnp.square(embeddings.astype(jnp.float32)), axis=1)) + 1e-06)
    scales = scales.reshape(block_total, BLK)
    block_ids = jnp.arange(block_total, dtype=jnp.int32)
    source_owner = block_ids // (N_WORKER * NB)
    source_worker = block_ids // NB % N_WORKER
    target_worker = routing[block_owner, source_worker, source_owner]
    groups = block_owner * N_WORKER + target_worker
    table = jnp.zeros((N_OWNER * N_WORKER, N_OWNER), jnp.int32)
    table = table.at[groups, source_owner].set(block_ids)
    diagonal = jnp.eye(member_rows, dtype=bool)

    def one_group(slots):
        members = blocks[slots].reshape(member_rows, D)
        member_labels = labels[slots].reshape(member_rows)
        member_scales = scales[slots].reshape(member_rows)
        products = jnp.dot(members, members.T, preferred_element_type=jnp.float32)
        cosine = products * member_scales[:, None] * member_scales[None, :] / D
        allowed = (member_labels[:, None] == member_labels[None, :]) & jnp.logical_not(diagonal)
        return lax.optimization_barrier(jnp.max(jnp.where(allowed, cosine, -1.0), axis=1)).reshape(N_OWNER, BLK)
    values = lax.map(one_group, table)
    result = jnp.zeros((block_total, BLK), jnp.float32)
    result = result.at[table.reshape(-1)].set(values.reshape(-1, BLK))
    return result.reshape(-1)
```

```python
import jax
import jax.numpy as jnp
from jax import lax
from jax.experimental import pallas as pl
from jax.experimental.pallas import tpu as pltpu
from jax.sharding import PartitionSpec as P

MESH = pl.DeviceIdType.MESH
CHUNKS = 8
ROWS = 16
WIDTH = 4096
TILE = 256
NEG = -3.0e38
KIND = "AABBCCDD"
Y_STEPS = ((1, 0), (3, 1), (2, 0), (1, 1), (3, 0), (2, 1), (0, 1))
O_STEPS = tuple((a, b) for a in range(4) for b in range(4) if (a, b) != (0, 0))
ARRIVALS = (0, 1, 2, 4, 6, 3, 5, 7)


def kernel(tab, emb, lab, out, r1, *scratch):
    sends = scratch[0:8]
    mids = scratch[8:16]
    (
        members, stage0, stage1, lab_a, lab_b, lab_c, lab_d, lab_e, label_rows, scale_rows, best_rows, lane_best,
        result, gathered, relayed, home, send_sem, recv_sem, local_sem, stage_sem,
        res_send, res_recv, home_send, home_recv,
    ) = scratch[16:]
    owner = lax.axis_index("owner")
    worker = lax.axis_index("worker")
    mz, mx = owner // 4, owner % 4
    my, mc = worker // 2, worker % 2

    def turn(value, step, size):
        return lax.rem(value + step, size)

    def owner_of(dz, dx):
        return turn(mz, dz, 4) * 4 + turn(mx, dx, 4)

    def worker_of(dy, dc):
        return turn(my, dy, 4) * 2 + turn(mc, dc, 2)

    barrier = pltpu.get_barrier_semaphore()
    for dz, dx in O_STEPS:
        pl.semaphore_signal(barrier, inc=1, device_id=(owner_of(dz, dx), worker), device_id_type=MESH)
    for dy, dc in Y_STEPS:
        pl.semaphore_signal(barrier, inc=1, device_id=(owner, worker_of(dy, dc)), device_id_type=MESH)

    def remote(src, dst, send, recv, to):
        return pltpu.make_async_remote_copy(
            src_ref=src, dst_ref=dst, send_sem=send, recv_sem=recv, device_id=to, device_id_type=MESH
        )

    def hop(axis, src, dst, n, stage):
        copies = []
        if axis == "z":
            for i, d in enumerate((1, 3, 2)):
                to = turn(mz, d, 4)
                copies.append(
                    remote(src.at[to], dst.at[mz], send_sem.at[n, stage, i], recv_sem.at[n, stage, i], (to * 4 + mx, worker))
                )
            here = (src.at[mz], dst.at[mz])
        elif axis == "x":
            for i, d in enumerate((1, 3, 2)):
                to = turn(mx, d, 4)
                copies.append(
                    remote(src.at[:, to], dst.at[:, mx], send_sem.at[n, stage, i], recv_sem.at[n, stage, i], (mz * 4 + to, worker))
                )
            here = (src.at[:, mx], dst.at[:, mx])
        else:
            for i, (dy, dc) in enumerate(Y_STEPS):
                to = worker_of(dy, dc)
                copies.append(
                    remote(
                        src.at[to // 2, pl.ds(2 * lax.rem(to, 2), 2)], dst.at[my, pl.ds(2 * mc, 2)],
                        send_sem.at[n, stage, i], recv_sem.at[n, stage, i], (owner, to),
                    )
                )
            here = (src.at[my, pl.ds(2 * mc, 2)], dst.at[my, pl.ds(2 * mc, 2)])
        copies.append(pltpu.make_async_copy(here[0], here[1], local_sem.at[n, stage]))
        return copies

    flying = {}

    def start(n, stage, axis, src, dst):
        flying[n, stage] = hop(axis, src, dst, n, stage)
        for copy in flying[n, stage]:
            copy.start()

    def wait(n, stage):
        for copy in flying[n, stage][:-1]:
            copy.wait_recv()
            copy.wait_send()
        flying[n, stage][-1].wait()

    def permute(row, src, dst, flat=False):
        def body(slot, carry):
            index = tab[row, slot]
            if flat:
                dst[slot >> 2, slot & 3] = src[index]
            else:
                dst[slot >> 2, slot & 3] = src[index >> 2, index & 3]
            return carry

        lax.fori_loop(0, 16, body, 0)

    def route(n):
        if n == CHUNKS:
            return (("z", lab_a, lab_b), ("x", lab_b, lab_c), ("y", lab_d, lab_e))
        s, r, m, f = sends[n], r1.at[n], mids[n], members.at[ARRIVALS.index(n)]
        return {
            "A": (("z", s, r), ("x", r, m), ("y", s, f)),
            "B": (("x", s, r), ("z", r, m), ("y", s, f)),
            "C": (("y", s, m), ("z", s, r), ("x", r, f)),
            "D": (("y", s, m), ("x", s, r), ("z", r, f)),
        }[KIND[n]]

    def go(n, stage):
        start(n, stage, *route(n)[stage])

    def middle(n):
        if n == CHUNKS:
            permute(2, lab_c, lab_d)
        else:
            permute(2 if KIND[n] in "AB" else 3, mids[n], sends[n])

    stages = (stage0, stage1)

    def fetch(n, at):
        return pltpu.make_async_copy(emb.at[:, pl.ds(ROWS * n, ROWS), :], stages[at], stage_sem.at[at])

    first = (0, 2, 4, 1, 3, 5, 6, 7)
    fetch(first[0], 0).start()
    fetch(first[1], 1).start()
    permute(0, lab, lab_a, flat=True)
    for i, n in enumerate(first):
        fetch(n, i % 2).wait()
        permute(0 if KIND[n] in "AB" else 1, stages[i % 2], sends[n], flat=True)
        if i + 2 < len(first):
            fetch(first[i + 2], i % 2).start()
        if i == 0:
            pl.semaphore_wait(barrier, len(O_STEPS) + len(Y_STEPS))
        if KIND[n] != "D":
            go(n, 0)
        if i == 2:
            go(CHUNKS, 0)

    lane = lax.broadcasted_iota(jnp.int32, (1, TILE), 1)
    eye = lax.broadcasted_iota(jnp.int32, (TILE, TILE), 0) == lax.broadcasted_iota(jnp.int32, (TILE, TILE), 1)

    def as_column(row):
        column = jnp.transpose(jnp.broadcast_to(row, (128, TILE)))
        return jnp.concatenate([column, column], axis=1)

    def product(a, b):
        return lax.dot_general(a, b, (((1,), (1,)), ((), ())), preferred_element_type=jnp.float32)

    def chunk_of(i):
        return members[i].reshape(TILE, WIDTH)

    def gram(i):
        n = ARRIVALS[i]
        row = jnp.zeros((1, TILE), jnp.float32)
        for slot in range(16):
            if KIND[n] in "AB":
                tile = lab_e[slot // 4, slot % 4]
            else:
                index = tab[4, slot]
                tile = lab_e[index >> 2, index & 3]
            row = jnp.where(lane // 16 == slot, tile[n : n + 1, :], row)
        label_rows[i] = jnp.broadcast_to(row, (8, TILE))
        labels = as_column(row)
        own = product(chunk_of(i), chunk_of(i))
        scale = lax.rsqrt(jnp.sum(jnp.where(eye, own, 0.0), axis=0, keepdims=True) / WIDTH + 1e-6)
        scale_rows[i] = jnp.broadcast_to(scale, (8, TILE))
        scales = as_column(scale)
        scored = jnp.where((labels == row) & jnp.logical_not(eye), own * scales, NEG)
        best_rows[i] = jnp.broadcast_to(jnp.max(scored, axis=0, keepdims=True), (8, TILE))
        lane_best[...] = jnp.full((TILE, 128), NEG, jnp.float32)

        def body(j, carry):
            other = product(chunk_of(i), chunk_of(j))
            match = labels == label_rows[j][0:1]
            down = jnp.max(jnp.where(match, other * scales, NEG), axis=0, keepdims=True)
            best_rows[j] = jnp.maximum(best_rows[j], jnp.broadcast_to(down, (8, TILE)))
            across = jnp.where(match, other * scale_rows[j][0:1], NEG)
            lane_best[...] = jnp.maximum(lane_best[...], jnp.maximum(across[:, :128], across[:, 128:]))
            return carry

        if i > 0:
            lax.fori_loop(0, i, body, 0)
            turned = jnp.max(jnp.transpose(lane_best[...]), axis=0, keepdims=True)
            best_rows[i] = jnp.maximum(best_rows[i], jnp.broadcast_to(turned, (8, TILE)))

    wait(0, 0); go(0, 1)
    wait(2, 0); go(2, 1)
    wait(4, 0); go(6, 0); middle(4)
    wait(8, 0); go(8, 1)
    wait(1, 0); go(1, 1)
    wait(3, 0); go(3, 1)
    wait(5, 0); go(7, 0); go(4, 1); middle(5)
    wait(0, 1); middle(0); go(0, 2)
    wait(8, 1); middle(8); go(8, 2)
    wait(2, 1); middle(2)
    wait(6, 0); middle(6); go(6, 1)
    wait(1, 1); middle(1); go(1, 2)
    go(5, 1)
    wait(3, 1); middle(3)
    wait(7, 0); middle(7); go(7, 1)
    wait(0, 2); go(2, 2)
    wait(4, 1); go(4, 2)
    wait(6, 1); go(6, 2)
    wait(8, 2); gram(0)
    wait(1, 2); go(3, 2)
    wait(5, 1); go(5, 2)
    wait(7, 1); go(7, 2)
    gram(1)
    wait(2, 2); gram(2)
    wait(4, 2); gram(3)
    wait(6, 2); gram(4)
    wait(3, 2); gram(5)
    wait(5, 2); gram(6)
    wait(7, 2); gram(7)

    for i, n in enumerate(ARRIVALS):
        result[n : n + 1, :] = jnp.maximum(best_rows[i][0:1] * scale_rows[i][0:1] / WIDTH, -1.0)
    back = [
        remote(result, gathered.at[worker], res_send.at[i], res_recv.at[i], (owner, worker_of(dy, dc)))
        for i, (dy, dc) in enumerate(Y_STEPS)
    ]
    for copy in back:
        copy.start()
    gathered[worker] = result[...]
    for copy in back:
        copy.wait()

    def relay(slot, carry):
        relayed[slot] = gathered[tab[5, slot]]
        return carry

    lax.fori_loop(0, 16, relay, 0)
    back = [
        remote(relayed.at[owner_of(dz, dx)], home.at[owner], home_send.at[i], home_recv.at[i], (owner_of(dz, dx), worker))
        for i, (dz, dx) in enumerate(O_STEPS)
    ]
    for copy in back:
        copy.start()
    home[owner] = relayed[owner]
    for copy in back:
        copy.wait()

    chunk = lax.broadcasted_iota(jnp.int32, (8, TILE), 0)
    place = lax.broadcasted_iota(jnp.int32, (8, TILE), 1) // 16
    chunk_half = lax.broadcasted_iota(jnp.int32, (8, 128), 0)
    place_half = lax.broadcasted_iota(jnp.int32, (8, 128), 1) // 16

    def unpack(block, carry):
        tile = home[tab[7, block]]
        kept = jnp.where(place == jnp.where(chunk < 4, tab[6, block], owner), tile, 0.0)
        kept = kept[:, :128] + kept[:, 128:]
        for shift in (64, 32, 16):
            kept = kept + pltpu.roll(kept, shift, 1)
        kept = jnp.where(place_half == chunk_half, kept, 0.0)
        out[pl.ds(block, 1), :] = jnp.sum(kept, axis=0, keepdims=True)
        return carry

    lax.fori_loop(0, 16, unpack, 0)


def tables(block_owner, routing):
    owner = lax.axis_index("owner")
    worker = lax.axis_index("worker")
    iota = jnp.arange(16, dtype=jnp.int32)
    before = iota[:, None] > iota[None, :]

    def rank(values):
        same = (values[:, None] == values[None, :]) & before
        return jnp.sum(same, axis=1, dtype=jnp.int32)

    def inverse(keys, payload):
        return jnp.sum(jnp.where(keys[None, :] == iota[:, None], payload[None, :], 0), axis=1, dtype=jnp.int32)

    sent = inverse(block_owner, iota)
    along_sources = routing[owner, worker, :]
    along_targets = routing[:, worker, owner]
    key_targets = 2 * along_targets + rank(along_targets)
    row1 = inverse(key_targets, sent)
    row2 = inverse(2 * along_sources + rank(along_sources), iota)

    def found(table):
        hit = table == worker
        count = jnp.cumsum(hit, axis=0, dtype=jnp.int32) - 1
        return jnp.sum(jnp.where(hit, 2 * jnp.arange(8, dtype=jnp.int32)[None, :] + count, 0), axis=1, dtype=jnp.int32)

    row3 = found(routing[:, :, owner])
    row4 = found(routing[owner].T)
    mine = routing[:, worker, :]
    earlier = (mine == along_targets[:, None]) & (iota[None, :] < owner)
    slot = 2 * worker + jnp.sum(earlier, axis=1, dtype=jnp.int32)
    row6 = jnp.sum(jnp.where(block_owner[:, None] == iota[None, :], slot[None, :], 0), axis=1, dtype=jnp.int32)
    return jnp.stack([sent, row1, row2, row3, row4, along_sources, row6, block_owner])


def shards(embeddings, row_cluster, block_owner, routing):
    labels = row_cluster.astype(jnp.float32).reshape(16, CHUNKS, ROWS)
    labels = jnp.tile(labels, (1, 1, 16))
    vmem = pl.BlockSpec(memory_space=pltpu.VMEM)
    anywhere = pl.BlockSpec(memory_space=pl.ANY)
    unit = (4, 4, ROWS, WIDTH)
    small = (4, 4, 8, TILE)
    out, _ = pl.pallas_call(
        kernel,
        out_shape=(
            jax.ShapeDtypeStruct((16, 128), jnp.float32),
            jax.ShapeDtypeStruct((CHUNKS, *unit), jnp.bfloat16),
        ),
        in_specs=[pl.BlockSpec(memory_space=pltpu.SMEM), anywhere, vmem],
        out_specs=(vmem, anywhere),
        scratch_shapes=[
            *[pltpu.VMEM(unit, jnp.bfloat16) for _ in range(8)],
            *[pltpu.VMEM(unit, jnp.bfloat16) for _ in range(8)],
            pltpu.VMEM((CHUNKS, *unit), jnp.bfloat16),
            *[pltpu.VMEM((16, ROWS, WIDTH), jnp.bfloat16) for _ in range(2)],
            *[pltpu.VMEM(small, jnp.float32) for _ in range(5)],
            *[pltpu.VMEM((CHUNKS, 8, TILE), jnp.float32) for _ in range(3)],
            pltpu.VMEM((TILE, 128), jnp.float32),
            pltpu.VMEM((8, TILE), jnp.float32),
            pltpu.VMEM((8, 8, TILE), jnp.float32),
            pltpu.VMEM((16, 8, TILE), jnp.float32),
            pltpu.VMEM((16, 8, TILE), jnp.float32),
            pltpu.SemaphoreType.DMA((CHUNKS + 1, 3, 7)),
            pltpu.SemaphoreType.DMA((CHUNKS + 1, 3, 7)),
            pltpu.SemaphoreType.DMA((CHUNKS + 1, 3)),
            pltpu.SemaphoreType.DMA((2,)),
            pltpu.SemaphoreType.DMA((7,)),
            pltpu.SemaphoreType.DMA((7,)),
            pltpu.SemaphoreType.DMA((15,)),
            pltpu.SemaphoreType.DMA((15,)),
        ],
        compiler_params=pltpu.CompilerParams(
            collective_id=0, has_side_effects=True, vmem_limit_bytes=62 * 2**20
        ),
        cost_estimate=pl.CostEstimate(flops=2 * 36 * 256 * 256 * 4096, bytes_accessed=64 * 2**20, transcendentals=2048),
    )(tables(block_owner, routing), embeddings.reshape(16, 128, WIDTH), labels)
    return out.reshape(-1)


def solution(mesh):
    placed = (P(("owner", "worker"), None), P(("owner", "worker")), P(("owner", "worker")), P())
    return jax.shard_map(
        shards, mesh=mesh, in_specs=placed, out_specs=P(("owner", "worker")), check_vma=False
    )
```

```python
import jax
import jax.numpy as jnp
from jax import lax
from jax.experimental import pallas as pl
from jax.experimental.pallas import tpu as pltpu
from jax.sharding import PartitionSpec as P

MESH = pl.DeviceIdType.MESH
CHUNKS = 8
HALVES = 2
UNITS = CHUNKS * HALVES
ROWS = 16
WIDTH = 4096
PART = WIDTH // HALVES
TILE = 256
NEG = -3.0e38
FLYING = 2
AXES = {"A": "zxy", "B": "xzy", "C": "yzx", "D": "yxz"}
Y_STEPS = ((1, 0), (3, 1), (2, 0), (1, 1), (3, 0), (2, 1), (0, 1))
O_STEPS = tuple((a, b) for a in range(4) for b in range(4) if (a, b) != (0, 0))
LATE = 5
LABELS = UNITS
SENT, FIRST, MID_SOURCE, MID_TARGET, PLACES, KEY, HOME = range(7)


def kind(unit):
    return "ABCD"[unit // 4]


def chunk_of_unit(unit):
    return unit // 2


def half_of_unit(unit):
    return unit % 2


def plan():
    steps = []
    queue = {"z": [], "x": [], "y": []}
    flying = {"z": [], "x": [], "y": []}
    free_at = {"z": 0, "x": 0, "y": 0}

    def fill(axis, now):
        while queue[axis] and len(flying[axis]) < FLYING:
            unit, stage = queue[axis].pop(0)
            free_at[axis] = max(free_at[axis], now) + 1
            flying[axis].append((free_at[axis], unit, stage))
            steps.append(("go", unit, stage))

    for sub in range(4):
        for letter in range(3):
            queue[AXES["ABCD"[letter]][0]].append((4 * letter + sub, 0))
    for sub in range(4):
        queue["y"].append((12 + sub, 0))
    for _ in range(FLYING):
        for axis in "zxy":
            unit, stage = queue[axis].pop(0)
            free_at[axis] += 1
            flying[axis].append((free_at[axis], unit, stage))
            steps.append(("go", unit, stage))
    steps.append(("ready",))
    while any(flying.values()):
        now, axis = min((flying[axis][0][0], "zxy".index(axis)) for axis in "zxy" if flying[axis])
        axis = "zxy"[axis]
        _, unit, stage = flying[axis].pop(0)
        steps.append(("wait", unit, stage))
        fill(axis, now)
        if stage == 2:
            steps.append(("arrived", unit))
            continue
        if stage == (1 if kind(unit) in "AB" else 0):
            steps.append(("middle", unit))
        following = AXES[kind(unit)][stage + 1]
        queue[following].append((unit, stage + 1))
        fill(following, now)
    return steps


STEPS = plan()
ARRIVALS = tuple(step[1] // 2 for step in STEPS if step[0] == "arrived" and step[1] % 2 == 1)


def kernel(owners, routing, emb, lab, out, r1, *scratch):
    sends = scratch[0:UNITS]
    mids = scratch[UNITS : 2 * UNITS]
    (
        members, stage0, stage1, lab_0, lab_a, lab_b, lab_c, lab_d, lab_e, label_rows, scale_rows, best_rows, lane_best, partial,
        result, gathered, relayed, home, tab, send_sem, recv_sem, local_sem, stage_sem,
        res_send, res_recv, home_send, home_recv,
    ) = scratch[2 * UNITS :]
    owner = lax.axis_index("owner")
    worker = lax.axis_index("worker")
    mz, mx = owner // 4, owner % 4
    my, mc = worker // 2, worker % 2

    def turn(value, step, size):
        return lax.rem(value + step, size)

    def owner_of(dz, dx):
        return turn(mz, dz, 4) * 4 + turn(mx, dx, 4)

    def worker_of(dy, dc):
        return turn(my, dy, 4) * 2 + turn(mc, dc, 2)

    barrier = pltpu.get_barrier_semaphore()
    for dz, dx in O_STEPS:
        pl.semaphore_signal(barrier, inc=1, device_id=(owner_of(dz, dx), worker), device_id_type=MESH)
    for dy, dc in Y_STEPS:
        pl.semaphore_signal(barrier, inc=1, device_id=(owner, worker_of(dy, dc)), device_id_type=MESH)

    def remote(src, dst, send, recv, to):
        return pltpu.make_async_remote_copy(
            src_ref=src, dst_ref=dst, send_sem=send, recv_sem=recv, device_id=to, device_id_type=MESH
        )

    def hop(axis, src, dst, n, stage):
        copies = []
        if axis == "z":
            for i, d in enumerate((1, 3, 2)):
                to = turn(mz, d, 4)
                copies.append(
                    remote(src.at[to], dst.at[mz], send_sem.at[n, stage, i], recv_sem.at[n, stage, i], (to * 4 + mx, worker))
                )
            here = (src.at[mz], dst.at[mz])
        elif axis == "x":
            for i, d in enumerate((1, 3, 2)):
                to = turn(mx, d, 4)
                copies.append(
                    remote(src.at[:, to], dst.at[:, mx], send_sem.at[n, stage, i], recv_sem.at[n, stage, i], (mz * 4 + to, worker))
                )
            here = (src.at[:, mx], dst.at[:, mx])
        else:
            for i, (dy, dc) in enumerate(Y_STEPS):
                to = worker_of(dy, dc)
                copies.append(
                    remote(
                        src.at[to // 2, pl.ds(2 * lax.rem(to, 2), 2)], dst.at[my, pl.ds(2 * mc, 2)],
                        send_sem.at[n, stage, i], recv_sem.at[n, stage, i], (owner, to),
                    )
                )
            here = (src.at[my, pl.ds(2 * mc, 2)], dst.at[my, pl.ds(2 * mc, 2)])
        copies.append(pltpu.make_async_copy(here[0], here[1], local_sem.at[n, stage]))
        return copies

    flying = {}

    def wait(n, stage):
        for copy in flying[n, stage][:-1]:
            copy.wait_recv()
            copy.wait_send()
        flying[n, stage][-1].wait()

    def permute(row, src, dst, flat=False):
        def body(slot, carry):
            index = tab[row, slot]
            if flat:
                dst[slot >> 2, slot & 3] = src[index]
            else:
                dst[slot >> 2, slot & 3] = src[index >> 2, index & 3]
            return carry

        lax.fori_loop(0, 16, body, 0)

    def route(n):
        if n == LABELS:
            return "zxy", ((lab_a, lab_b), (lab_b, lab_c), (lab_d, lab_e))
        s, r, m = sends[n], r1.at[n], mids[n]
        f = members.at[half_of_unit(n), ARRIVALS.index(chunk_of_unit(n))]
        return AXES[kind(n)], ((s, r), (r, m), (s, f)) if kind(n) in "AB" else ((s, m), (s, r), (r, f))

    def go(n, stage):
        axes, ends = route(n)
        flying[n, stage] = hop(axes[stage], *ends[stage], n, stage)
        for copy in flying[n, stage]:
            copy.start()

    def middle(n):
        if n == LABELS:
            permute(MID_SOURCE, lab_c, lab_d)
        else:
            permute(MID_SOURCE if kind(n) in "AB" else MID_TARGET, mids[n], sends[n])

    def invert(row, keys, payload):
        def body(slot, carry):
            found = jnp.int32(0)
            for i in range(16):
                found += jnp.where(keys(i) == slot, payload(i), 0)
            tab[row, slot] = found & 15
            return carry

        lax.fori_loop(0, 16, body, 0)

    def ranked(row, values):
        def body(slot, carry):
            value = values(slot)
            count = jnp.int32(0)
            for i in range(16):
                count += jnp.where((values(i) == value) & (i < slot), 1, 0)
            tab[row, slot] = 2 * value + count
            return carry

        lax.fori_loop(0, 16, body, 0)

    def find(row, values):
        def body(slot, counts):
            found = jnp.int32(0)
            after = []
            for w in range(8):
                hit = values(slot, w) == worker
                found += jnp.where(hit, 2 * w + counts[w], 0)
                after.append(counts[w] + jnp.where(hit, 1, 0))
            tab[row, slot] = found & 15
            return tuple(after)

        lax.fori_loop(0, 16, body, tuple(jnp.int32(0) for _ in range(8)))

    def home_slots():
        def body(slot, carry):
            target = owners[slot]
            mine = routing[target, worker, owner]
            count = jnp.int32(0)
            for i in range(16):
                count += jnp.where((routing[target, worker, i] == mine) & (i < owner), 1, 0)
            tab[HOME, slot] = 2 * worker + count
            return carry

        lax.fori_loop(0, 16, body, 0)

    stages = (stage0, stage1)

    def fetch(n, at):
        columns = pl.ds(PART * half_of_unit(n), PART)
        return pltpu.make_async_copy(
            emb.at[:, pl.ds(ROWS * chunk_of_unit(n), ROWS), columns], stages[at], stage_sem.at[at]
        )

    lane = lax.broadcasted_iota(jnp.int32, (1, TILE), 1)
    eye = lax.broadcasted_iota(jnp.int32, (TILE, TILE), 0) == lax.broadcasted_iota(jnp.int32, (TILE, TILE), 1)
    chunk_half = lax.broadcasted_iota(jnp.int32, (8, 128), 0)
    place_half = lax.broadcasted_iota(jnp.int32, (8, 128), 1) // 16
    on_place = place_half == chunk_half

    def spread(x):
        for shift in (64, 32, 16):
            x = x + pltpu.roll(x, shift, 1)
        return x

    def label_tiles():
        for block in range(16):
            row = lab[block : block + 1, :].astype(jnp.float32)
            lab_0[block] = spread(jnp.where(on_place, row, 0.0))

    steps = STEPS
    order = [step[1] for step in steps if step[0] == "go" and step[2] == 0]
    fetch(order[0], 0).start()
    fetch(order[1], 1).start()
    invert(SENT, lambda i: owners[i], lambda i: i)
    prepared = []

    def prepare(n):
        at = len(prepared)
        prepared.append(n)
        fetch(n, at % 2).wait()
        permute(SENT if kind(n) in "AB" else FIRST, stages[at % 2], sends[n], flat=True)
        if at + 2 < UNITS:
            fetch(order[at + 2], at % 2).start()

    def as_column(row):
        column = jnp.transpose(jnp.broadcast_to(row, (128, TILE)))
        return jnp.concatenate([column, column], axis=1)

    def product(i, j, half):
        a = members[half, i].reshape(TILE, PART)
        b = members[half, j].reshape(TILE, PART)
        return lax.dot_general(a, b, (((1,), (1,)), ((), ())), preferred_element_type=jnp.float32)

    def base(i):
        return sum(range(LATE + 1, i + 1))

    def gram_first(i):
        def body(j, carry):
            partial[base(i) + j] = product(i, j, 0)
            return carry

        lax.fori_loop(0, i + 1, body, 0)

    def full(i, j):
        if i >= LATE:
            return partial[base(i) + j] + product(i, j, 1)
        return product(i, j, 0) + product(i, j, 1)

    def gram_labels(i):
        n = ARRIVALS[i]
        row = jnp.zeros((1, TILE), jnp.float32)
        for slot in range(16):
            if n < 4:
                tile = lab_e[slot // 4, slot % 4]
            else:
                index = tab[PLACES, slot]
                tile = lab_e[index >> 2, index & 3]
            piece = tile[n : n + 1, :]
            row = jnp.where(lane // 16 == slot, jnp.concatenate([piece, piece], axis=1), row)
        label_rows[i] = jnp.broadcast_to(row, (8, TILE))

    def gram(i):
        row = label_rows[i][0:1]
        labels = as_column(row)
        own = full(i, i)
        scale = lax.rsqrt(jnp.sum(jnp.where(eye, own, 0.0), axis=0, keepdims=True) / WIDTH + 1e-6)
        scale_rows[i] = jnp.broadcast_to(scale, (8, TILE))
        scales = as_column(scale)
        scored = jnp.where((labels == row) & jnp.logical_not(eye), own * scales, NEG)
        best_rows[i] = jnp.broadcast_to(jnp.max(scored, axis=0, keepdims=True), (8, TILE))
        lane_best[...] = jnp.full((TILE, 128), NEG, jnp.float32)

        def body(j, carry):
            other = full(i, j)
            match = labels == label_rows[j][0:1]
            down = jnp.max(jnp.where(match, other * scales, NEG), axis=0, keepdims=True)
            best_rows[j] = jnp.maximum(best_rows[j], jnp.broadcast_to(down, (8, TILE)))
            across = jnp.where(match, other * scale_rows[j][0:1], NEG)
            lane_best[...] = jnp.maximum(lane_best[...], jnp.maximum(across[:, :128], across[:, 128:]))
            return carry

        if i > 0:
            lax.fori_loop(0, i, body, 0)
            turned = jnp.max(jnp.transpose(lane_best[...]), axis=0, keepdims=True)
            best_rows[i] = jnp.maximum(best_rows[i], jnp.broadcast_to(turned, (8, TILE)))

    greeted = []
    arrived = set()
    for step in steps:
        if step[0] == "go":
            _, n, stage = step
            if stage == 0 and n not in prepared:
                if kind(n) in "CD" and not any(kind(m) in "CD" for m in prepared):
                    ranked(KEY, lambda i: routing[i, worker, owner])
                    invert(FIRST, lambda i: tab[KEY, i], lambda i: tab[SENT, i])
                prepare(n)
            if not greeted:
                greeted.append(True)
                pl.semaphore_wait(barrier, len(O_STEPS) + len(Y_STEPS))
            go(n, stage)
        elif step[0] == "ready":
            label_tiles()
            permute(SENT, lab_0, lab_a, flat=True)
            go(LABELS, 0)
            ranked(KEY, lambda i: routing[owner, worker, i])
            invert(MID_SOURCE, lambda i: tab[KEY, i], lambda i: i)
            find(MID_TARGET, lambda i, w: routing[i, w, owner])
            find(PLACES, lambda i, w: routing[owner, w, i])
            home_slots()
            while len(prepared) < UNITS:
                prepare(order[len(prepared)])
        elif step[0] == "wait":
            _, n, stage = step
            wait(n, stage)
            if kind(n) == "A" and n % 4 == 1 and stage < 2:
                wait(LABELS, stage)
                if stage == 1:
                    middle(LABELS)
                go(LABELS, stage + 1)
        elif step[0] == "middle":
            middle(step[1])
        else:
            n = step[1]
            if not arrived:
                wait(LABELS, 2)
                for i in range(CHUNKS):
                    gram_labels(i)
            arrived.add(n)
            i = ARRIVALS.index(chunk_of_unit(n))
            if half_of_unit(n) == 1 or i >= LATE:
                assert all(2 * m + h in arrived for m in ARRIVALS[: i + 1] for h in range(half_of_unit(n) + 1)), "order"
            if half_of_unit(n) == 1:
                gram(i)
            elif i >= LATE:
                gram_first(i)

    for i, n in enumerate(ARRIVALS):
        result[n : n + 1, :] = jnp.maximum(best_rows[i][0:1] * scale_rows[i][0:1] / WIDTH, -1.0)
    back = [
        remote(result, gathered.at[worker], res_send.at[i], res_recv.at[i], (owner, worker_of(dy, dc)))
        for i, (dy, dc) in enumerate(Y_STEPS)
    ]
    for copy in back:
        copy.start()
    gathered[worker] = result[...]
    for copy in back:
        copy.wait()
    for slot in range(16):
        relayed[slot] = gathered[routing[owner, worker, slot]]
    back = [
        remote(relayed.at[owner_of(dz, dx)], home.at[owner], home_send.at[i], home_recv.at[i], (owner_of(dz, dx), worker))
        for i, (dz, dx) in enumerate(O_STEPS)
    ]
    for copy in back:
        copy.start()
    home[owner] = relayed[owner]
    for copy in back:
        copy.wait()

    chunk = lax.broadcasted_iota(jnp.int32, (8, TILE), 0)
    place = lax.broadcasted_iota(jnp.int32, (8, TILE), 1) // 16
    kept = []
    for block in range(16):
        tile = home[owners[block]]
        tile = jnp.where(place == jnp.where(chunk < 4, tab[HOME, block], owner), tile, 0.0)
        kept.append(tile[:, :128] + tile[:, 128:])
    for block in range(16):
        tile = jnp.where(on_place, spread(kept[block]), 0.0)
        out[block : block + 1, :] = jnp.sum(tile, axis=0, keepdims=True)


def shards(embeddings, row_cluster, block_owner, routing):
    vmem = pl.BlockSpec(memory_space=pltpu.VMEM)
    smem = pl.BlockSpec(memory_space=pltpu.SMEM)
    anywhere = pl.BlockSpec(memory_space=pl.ANY)
    unit = (4, 4, ROWS, PART)
    small = (4, 4, 8, 128)
    late = sum(range(LATE + 1, CHUNKS + 1))
    out, _ = pl.pallas_call(
        kernel,
        out_shape=(
            jax.ShapeDtypeStruct((16, 128), jnp.float32),
            jax.ShapeDtypeStruct((UNITS, *unit), jnp.bfloat16),
        ),
        in_specs=[smem, smem, anywhere, vmem],
        out_specs=(vmem, anywhere),
        scratch_shapes=[
            *[pltpu.VMEM(unit, jnp.bfloat16) for _ in range(UNITS)],
            *[pltpu.VMEM(unit, jnp.bfloat16) for _ in range(UNITS)],
            pltpu.VMEM((HALVES, CHUNKS, *unit), jnp.bfloat16),
            *[pltpu.VMEM((16, ROWS, PART), jnp.bfloat16) for _ in range(2)],
            pltpu.VMEM((16, 8, 128), jnp.float32),
            *[pltpu.VMEM(small, jnp.float32) for _ in range(5)],
            *[pltpu.VMEM((CHUNKS, 8, TILE), jnp.float32) for _ in range(3)],
            pltpu.VMEM((TILE, 128), jnp.float32),
            pltpu.VMEM((late, TILE, TILE), jnp.float32),
            pltpu.VMEM((8, TILE), jnp.float32),
            pltpu.VMEM((8, 8, TILE), jnp.float32),
            pltpu.VMEM((16, 8, TILE), jnp.float32),
            pltpu.VMEM((16, 8, TILE), jnp.float32),
            pltpu.SMEM((8, 16), jnp.int32),
            pltpu.SemaphoreType.DMA((UNITS + 1, 3, 7)),
            pltpu.SemaphoreType.DMA((UNITS + 1, 3, 7)),
            pltpu.SemaphoreType.DMA((UNITS + 1, 3)),
            pltpu.SemaphoreType.DMA((2,)),
            pltpu.SemaphoreType.DMA((7,)),
            pltpu.SemaphoreType.DMA((7,)),
            pltpu.SemaphoreType.DMA((15,)),
            pltpu.SemaphoreType.DMA((15,)),
        ],
        compiler_params=pltpu.CompilerParams(
            collective_id=0, has_side_effects=True, vmem_limit_bytes=62 * 2**20
        ),
        cost_estimate=pl.CostEstimate(flops=2 * 36 * 256 * 256 * 4096, bytes_accessed=64 * 2**20, transcendentals=2048),
    )(block_owner, routing, embeddings.reshape(16, 128, WIDTH), row_cluster.reshape(16, 128))
    return out.reshape(-1)


def solution(mesh):
    placed = (P(("owner", "worker"), None), P(("owner", "worker")), P(("owner", "worker")), P())
    return jax.shard_map(
        shards, mesh=mesh, in_specs=placed, out_specs=P(("owner", "worker")), check_vma=False
    )
```

```python
import jax
import jax.numpy as jnp
from jax import lax
from jax.experimental import pallas as pl
from jax.experimental.pallas import tpu as pltpu
from jax.sharding import PartitionSpec as P

MESH = pl.DeviceIdType.MESH
CHUNKS = 8
PARTS = 5
UNITS = 4 * PARTS
ROWS = 16
WIDTH = 4096
WIDEST = 2048
STAGES = 3
CUTS = ((0, 2048), (2048, 2048), (0, 2048), (2048, 1280), (3328, 768))
TILE = 256
NEG = -3.0e38
FAR = -1.0e30
FLYING = 2
AXES = {"A": "zxy", "B": "xzy", "C": "yzx", "D": "yxz"}
Y_STEPS = ((1, 0), (3, 1), (2, 0), (1, 1), (3, 0), (2, 1), (0, 1))
O_STEPS = tuple((a, b) for a in range(4) for b in range(4) if (a, b) != (0, 0))
LATE = 5
LABELS = UNITS
SENT, FIRST, MID_SOURCE, MID_TARGET, PLACES, KEY, HOME = range(7)


def kind(unit):
    return "ABCD"[unit // PARTS]


def chunk_of_unit(unit):
    return 2 * (unit // PARTS) + (unit % PARTS) // 2 - (unit % PARTS) // 4


def columns_of(unit):
    return CUTS[unit % PARTS]


def plan():
    steps = []
    queue = {"z": [], "x": [], "y": []}
    flying = {"z": [], "x": [], "y": []}
    free_at = {"z": 0, "x": 0, "y": 0}

    def fill(axis, now):
        while queue[axis] and len(flying[axis]) < FLYING:
            unit, stage = queue[axis].pop(0)
            free_at[axis] = max(free_at[axis], now) + columns_of(unit)[1]
            flying[axis].append((free_at[axis], unit, stage))
            steps.append(("go", unit, stage))

    for sub in range(PARTS):
        for letter in range(3):
            queue[AXES["ABCD"[letter]][0]].append((PARTS * letter + sub, 0))
    for sub in range(PARTS):
        queue["y"].append((3 * PARTS + sub, 0))
    for _ in range(FLYING):
        for axis in "zxy":
            unit, stage = queue[axis].pop(0)
            free_at[axis] += columns_of(unit)[1]
            flying[axis].append((free_at[axis], unit, stage))
            steps.append(("go", unit, stage))
    steps.append(("ready",))
    while any(flying.values()):
        now, axis = min((flying[axis][0][0], "zxy".index(axis)) for axis in "zxy" if flying[axis])
        axis = "zxy"[axis]
        _, unit, stage = flying[axis].pop(0)
        steps.append(("wait", unit, stage))
        fill(axis, now)
        if stage == 2:
            steps.append(("arrived", unit))
            continue
        if stage == (1 if kind(unit) in "AB" else 0):
            steps.append(("middle", unit))
        following = AXES[kind(unit)][stage + 1]
        queue[following].append((unit, stage + 1))
        fill(following, now)
    return steps


STEPS = plan()
ARRIVALS = tuple(chunk_of_unit(step[1]) for step in STEPS if step[0] == "arrived" and step[1] % PARTS in (1, 4))


def kernel(owners, routing_far, emb, lab_far, out, r1, *scratch):
    sends = scratch[0:UNITS]
    mids = scratch[UNITS : 2 * UNITS]
    (
        members, stage0, stage1, stage2, lab, routing, lab_0, lab_a, lab_b, lab_c, lab_d, lab_e, label_rows, scale_rows, best_rows, lane_best, partial, rest,
        result, gathered, relayed, home, tab, send_sem, recv_sem, local_sem, stage_sem, table_sem, back_sem,
    ) = scratch[2 * UNITS :]
    owner = lax.axis_index("owner")
    worker = lax.axis_index("worker")
    mz, mx = owner // 4, owner % 4
    my, mc = worker // 2, worker % 2

    def turn(value, step, size):
        return lax.rem(value + step, size)

    def owner_of(dz, dx):
        return turn(mz, dz, 4) * 4 + turn(mx, dx, 4)

    def worker_of(dy, dc):
        return turn(my, dy, 4) * 2 + turn(mc, dc, 2)

    stages = (stage0, stage1, stage2)

    def fetch(n, at):
        first, width = columns_of(n)
        return pltpu.make_async_copy(
            emb.at[:, pl.ds(ROWS * chunk_of_unit(n), ROWS), pl.ds(first, width)],
            stages[at].at[:, :, pl.ds(0, width)],
            stage_sem.at[at],
        )

    steps = STEPS
    order = [step[1] for step in steps if step[0] == "go" and step[2] == 0]
    for at in range(STAGES):
        fetch(order[at], at).start()
    routing_copy = pltpu.make_async_copy(routing_far, routing, table_sem.at[0])
    routing_copy.start()
    lab_copy = pltpu.make_async_copy(lab_far, lab, table_sem.at[1])
    lab_copy.start()
    barrier = pltpu.get_barrier_semaphore()
    for dz, dx in O_STEPS:
        pl.semaphore_signal(barrier, inc=1, device_id=(owner_of(dz, dx), worker), device_id_type=MESH)
    for dy, dc in Y_STEPS:
        pl.semaphore_signal(barrier, inc=1, device_id=(owner, worker_of(dy, dc)), device_id_type=MESH)

    def remote(src, dst, send, recv, to):
        return pltpu.make_async_remote_copy(
            src_ref=src, dst_ref=dst, send_sem=send, recv_sem=recv, device_id=to, device_id_type=MESH
        )

    def hop(axis, src, dst, send, recv, local):
        copies = []
        if axis == "z":
            for d in (1, 3, 2):
                to = turn(mz, d, 4)
                copies.append(remote(src.at[to], dst.at[mz], send, recv, (to * 4 + mx, worker)))
            here = (src.at[mz], dst.at[mz])
        elif axis == "x":
            for d in (1, 3, 2):
                to = turn(mx, d, 4)
                copies.append(remote(src.at[:, to], dst.at[:, mx], send, recv, (mz * 4 + to, worker)))
            here = (src.at[:, mx], dst.at[:, mx])
        else:
            for dy, dc in Y_STEPS:
                to = worker_of(dy, dc)
                copies.append(
                    remote(src.at[to // 2, pl.ds(2 * lax.rem(to, 2), 2)], dst.at[my, pl.ds(2 * mc, 2)], send, recv, (owner, to))
                )
            here = (src.at[my, pl.ds(2 * mc, 2)], dst.at[my, pl.ds(2 * mc, 2)])
        copies.append(pltpu.make_async_copy(here[0], here[1], local))
        return copies

    flying = {}
    started = {"z": 0, "x": 0, "y": 0}

    def all_of(like, sem):
        pltpu.make_async_copy(like, like, sem).wait()

    def wait(n, stage):
        axis, local, place = flying.pop((n, stage))
        like = size_of(n, axis)
        all_of(like, recv_sem.at[n, stage])
        local.wait()

    def size_of(n, axis):
        blocks = 14 if axis == "y" else 12
        return lab_0.at[pl.ds(0, blocks)] if n == LABELS else stage0.at[pl.ds(0, blocks), :, pl.ds(0, columns_of(n)[1])]

    sending = {}

    def sent(place):
        if place in sending:
            n, axis = sending.pop(place)
            all_of(size_of(n, axis), send_sem.at[place])

    def permute(row, src, dst, flat=False, width=None):
        def body(slot, carry):
            index = tab[row, slot]
            if width is not None:
                dst[slot >> 2, slot & 3] = src[index, :, pl.ds(0, width)]
            elif flat:
                dst[slot >> 2, slot & 3] = src[index]
            else:
                dst[slot >> 2, slot & 3] = src[index >> 2, index & 3]
            return carry

        lax.fori_loop(0, 16, body, 0)

    def route(n):
        if n == LABELS:
            return "zxy", ((lab_a, lab_b), (lab_b, lab_c), (lab_d, lab_e))
        columns = pl.ds(*columns_of(n))
        s, r, m = sends[n], r1.at[chunk_of_unit(n), :, :, :, columns], mids[n]
        f = members.at[ARRIVALS.index(chunk_of_unit(n)), :, :, :, columns]
        return AXES[kind(n)], ((s, r), (r, m), (s, f)) if kind(n) in "AB" else ((s, m), (s, r), (r, f))

    def go(n, stage):
        axes, ends = route(n)
        axis = axes[stage]
        if n == LABELS:
            place = (3, stage)
        else:
            place = ("zxy".index(axis), started[axis] % (FLYING + 1))
            started[axis] += 1
        sent(place)
        sending[place] = (n, axis)
        copies = hop(axis, *ends[stage], send_sem.at[place], recv_sem.at[n, stage], local_sem.at[place])
        flying[n, stage] = (axis, copies[-1], place)
        for copy in copies:
            copy.start()

    def middle(n):
        for place in [place for place in sending if sending[place][0] == n]:
            sent(place)
        if n == LABELS:
            permute(MID_SOURCE, lab_c, lab_d)
        else:
            permute(MID_SOURCE if kind(n) in "AB" else MID_TARGET, mids[n], sends[n])

    def invert(row, keys, payload):
        def body(slot, carry):
            found = jnp.int32(0)
            for i in range(16):
                found += jnp.where(keys(i) == slot, payload(i), 0)
            tab[row, slot] = found & 15
            return carry

        lax.fori_loop(0, 16, body, 0)

    def ranked(row, values):
        def body(slot, carry):
            value = values(slot)
            count = jnp.int32(0)
            for i in range(16):
                count += jnp.where((values(i) == value) & (i < slot), 1, 0)
            tab[row, slot] = 2 * value + count
            return carry

        lax.fori_loop(0, 16, body, 0)

    def find(row, values):
        def body(slot, counts):
            found = jnp.int32(0)
            after = []
            for w in range(8):
                hit = values(slot, w) == worker
                found += jnp.where(hit, 2 * w + counts[w], 0)
                after.append(counts[w] + jnp.where(hit, 1, 0))
            tab[row, slot] = found & 15
            return tuple(after)

        lax.fori_loop(0, 16, body, tuple(jnp.int32(0) for _ in range(8)))

    def home_slots():
        def body(slot, carry):
            target = owners[slot]
            mine = routing[target, worker, owner]
            count = jnp.int32(0)
            for i in range(16):
                count += jnp.where((routing[target, worker, i] == mine) & (i < owner), 1, 0)
            tab[HOME, slot] = 2 * worker + count
            return carry

        lax.fori_loop(0, 16, body, 0)

    lane = lax.broadcasted_iota(jnp.int32, (1, TILE), 1)
    eye = lax.broadcasted_iota(jnp.int32, (TILE, TILE), 0) == lax.broadcasted_iota(jnp.int32, (TILE, TILE), 1)
    chunk_half = lax.broadcasted_iota(jnp.int32, (8, 128), 0)
    place_half = lax.broadcasted_iota(jnp.int32, (8, 128), 1) // 16
    on_place = place_half == chunk_half

    def spread(x):
        for shift in (64, 32, 16):
            x = x + pltpu.roll(x, shift, 1)
        return x

    def label_tiles():
        for block in range(16):
            row = lab[block : block + 1, :].astype(jnp.float32)
            lab_0[block] = spread(jnp.where(on_place, row, 0.0))

    invert(SENT, lambda i: owners[i], lambda i: i)
    prepared = []

    def prepare(n):
        at = len(prepared)
        prepared.append(n)
        fetch(n, at % STAGES).wait()
        permute(SENT if kind(n) in "AB" else FIRST, stages[at % STAGES], sends[n], width=columns_of(n)[1])
        if at + STAGES < UNITS:
            fetch(order[at + STAGES], at % STAGES).start()

    def as_column(row):
        column = jnp.transpose(jnp.broadcast_to(row, (128, TILE)))
        return jnp.concatenate([column, column], axis=1)

    def product(first, count, j, columns):
        a = members[first : first + count, :, :, :, columns].reshape(count * TILE, columns.stop - columns.start)
        b = members[j, :, :, :, columns].reshape(TILE, columns.stop - columns.start)
        return lax.dot_general(a, b, (((1,), (1,)), ((), ())), preferred_element_type=jnp.float32)

    whole = slice(0, WIDTH)
    late_count = CHUNKS - LATE

    def part(level):
        first, width = CUTS[2 + level]
        return slice(first, first + width)

    def wide(at):
        column = rest[at * TILE : (at + 1) * TILE]
        return jnp.concatenate([column, column], axis=1)

    def keep(x, labels, j):
        return jnp.where(labels == label_rows[j][0:1], x, FAR)

    def late_products(level):
        if level == 0:
            for at in range(late_count):
                rest[at * TILE : (at + 1) * TILE] = as_column(label_rows[LATE + at][0:1])[:, :128]

        def body(j, carry):
            total = product(LATE, late_count, j, part(level))
            for at in range(late_count):
                rows = slice(at * TILE, (at + 1) * TILE)
                if level == 0:
                    partial[j, rows] = keep(total[rows], wide(at), j)
                else:
                    partial[j, rows] = partial[j, rows] + total[rows]
            return carry

        lax.fori_loop(0, LATE, body, 0)
        for j in range(LATE, CHUNKS):
            total = product(j, CHUNKS - j, j, part(level))
            for i in range(j, CHUNKS):
                rows, own = slice((i - LATE) * TILE, (i - LATE + 1) * TILE), total[(i - j) * TILE : (i - j + 1) * TILE]
                if level > 0:
                    own = own + partial[j, rows]
                elif i > j:
                    own = keep(own, wide(i - LATE), j)
                partial[j, rows] = own

    def gram_labels(i):
        n = ARRIVALS[i]
        row = jnp.zeros((1, TILE), jnp.float32)
        for slot in range(16):
            if n < 4:
                tile = lab_e[slot // 4, slot % 4]
            else:
                index = tab[PLACES, slot]
                tile = lab_e[index >> 2, index & 3]
            piece = tile[n : n + 1, :]
            row = jnp.where(lane // 16 == slot, jnp.concatenate([piece, piece], axis=1), row)
        label_rows[i] = jnp.broadcast_to(row, (8, TILE))

    def own_scores(i, own):
        row = label_rows[i][0:1]
        labels = as_column(row)
        scale = lax.rsqrt(jnp.sum(jnp.where(eye, own, 0.0), axis=0, keepdims=True) / WIDTH + 1e-6)
        scale_rows[i] = jnp.broadcast_to(scale, (8, TILE))
        scales = as_column(scale)
        scored = jnp.where((labels == row) & jnp.logical_not(eye), own * scales, NEG)
        best_rows[i] = jnp.broadcast_to(jnp.max(scored, axis=0, keepdims=True), (8, TILE))
        return labels, scales

    def pair(other, scales, j):
        down = jnp.max(other * scales, axis=0, keepdims=True)
        best_rows[j] = jnp.maximum(best_rows[j], jnp.broadcast_to(down, (8, TILE)))
        across = other * scale_rows[j][0:1]
        return jnp.maximum(across[:, :128], across[:, 128:])

    def settle(i, at):
        turned = jnp.max(jnp.transpose(lane_best[at]), axis=0, keepdims=True)
        best_rows[i] = jnp.maximum(best_rows[i], jnp.broadcast_to(turned, (8, TILE)))

    def gram(i):
        labels, scales = own_scores(i, product(i, 1, i, whole))
        lane_best[0] = jnp.full((TILE, 128), NEG, jnp.float32)

        def body(j, carry):
            lane_best[0] = jnp.maximum(lane_best[0], pair(keep(product(i, 1, j, whole), labels, j), scales, j))
            return carry

        if i > 0:
            lax.fori_loop(0, i, body, 0)
            settle(i, 0)

    def late_gram():
        last = part(2)
        scales = [None] * late_count
        for at in range(late_count):
            lane_best[at] = jnp.full((TILE, 128), NEG, jnp.float32)
        for j in range(LATE, CHUNKS):
            at = j - LATE
            total = partial[j, at * TILE :] + product(j, CHUNKS - j, j, last)
            _, scales[at] = own_scores(j, total[:TILE])
            rest[at * TILE : (at + 1) * TILE] = scales[at][:, :128]
            partial[j, at * TILE :] = total
        for j in range(LATE, CHUNKS):
            for i in range(j + 1, CHUNKS):
                at = i - LATE
                lane_best[at] = jnp.maximum(lane_best[at], pair(partial[j, at * TILE : (at + 1) * TILE], scales[at], j))

        def body(j, carry):
            total = partial[j] + product(LATE, late_count, j, last)
            for at in range(late_count):
                lane_best[at] = jnp.maximum(lane_best[at], pair(total[at * TILE : (at + 1) * TILE], wide(at), j))
            return carry

        lax.fori_loop(0, LATE, body, 0)
        for at in range(late_count):
            settle(LATE + at, at)

    greeted = []
    done = []
    arrived = set()
    for step in steps:
        if step[0] == "go":
            _, n, stage = step
            if stage == 0 and n not in prepared:
                if kind(n) in "CD" and not any(kind(m) in "CD" for m in prepared):
                    routing_copy.wait()
                    ranked(KEY, lambda i: routing[i, worker, owner])
                    invert(FIRST, lambda i: tab[KEY, i], lambda i: tab[SENT, i])
                prepare(n)
            if not greeted:
                greeted.append(True)
                pl.semaphore_wait(barrier, len(O_STEPS) + len(Y_STEPS))
            go(n, stage)
        elif step[0] == "ready":
            lab_copy.wait()
            label_tiles()
            permute(SENT, lab_0, lab_a, flat=True)
            go(LABELS, 0)
            ranked(KEY, lambda i: routing[owner, worker, i])
            invert(MID_SOURCE, lambda i: tab[KEY, i], lambda i: i)
            find(MID_TARGET, lambda i, w: routing[i, w, owner])
            find(PLACES, lambda i, w: routing[owner, w, i])
            home_slots()
            while len(prepared) < UNITS:
                prepare(order[len(prepared)])
        elif step[0] == "wait":
            _, n, stage = step
            wait(n, stage)
            if n == 1 and stage < 2:
                wait(LABELS, stage)
                if stage == 1:
                    middle(LABELS)
                go(LABELS, stage + 1)
        elif step[0] == "middle":
            middle(step[1])
        else:
            n = step[1]
            if not arrived:
                wait(LABELS, 2)
                for i in range(CHUNKS):
                    gram_labels(i)
            arrived.add(n)
            i = ARRIVALS.index(chunk_of_unit(n))
            if n % PARTS in (1, 4) and i < LATE:
                assert all(m in arrived for m in range(UNITS) if chunk_of_unit(m) in ARRIVALS[: i + 1]), "order"
                gram(i)
            while len(done) < 3:
                level = len(done)
                after = {m for m in range(UNITS) if chunk_of_unit(m) in ARRIVALS[LATE:] and m % PARTS > 2 + level}
                if arrived | after != set(range(UNITS)):
                    break
                done.append(level)
                if level < 2:
                    late_products(level)
                else:
                    late_gram()
    assert len(done) == 3, "order"

    for i, n in enumerate(ARRIVALS):
        result[n : n + 1, :] = jnp.maximum(best_rows[i][0:1] * scale_rows[i][0:1] / WIDTH, -1.0)
    for dy, dc in Y_STEPS:
        remote(result, gathered.at[worker], back_sem.at[0], back_sem.at[1], (owner, worker_of(dy, dc))).start()
    gathered[worker] = result[...]
    all_of(gathered.at[pl.ds(0, 7)], back_sem.at[1])
    for slot in range(16):
        relayed[slot] = gathered[routing[owner, worker, slot]]
    for dz, dx in O_STEPS:
        to = owner_of(dz, dx)
        remote(relayed.at[to], home.at[owner], back_sem.at[2], back_sem.at[3], (to, worker)).start()
    home[owner] = relayed[owner]
    all_of(home.at[pl.ds(0, 15)], back_sem.at[3])

    chunk = lax.broadcasted_iota(jnp.int32, (8, TILE), 0)
    place = lax.broadcasted_iota(jnp.int32, (8, TILE), 1) // 16
    kept = []
    for block in range(16):
        tile = home[owners[block]]
        tile = jnp.where(place == jnp.where(chunk < 4, tab[HOME, block], owner), tile, 0.0)
        kept.append(tile[:, :128] + tile[:, 128:])
    for block in range(16):
        tile = jnp.where(on_place, spread(kept[block]), 0.0)
        out[block : block + 1, :] = jnp.sum(tile, axis=0, keepdims=True)
    all_of(gathered.at[pl.ds(0, 7)], back_sem.at[0])
    all_of(home.at[pl.ds(0, 15)], back_sem.at[2])
    for place in list(sending):
        sent(place)


def shards(embeddings, row_cluster, block_owner, routing):
    vmem = pl.BlockSpec(memory_space=pltpu.VMEM)
    smem = pl.BlockSpec(memory_space=pltpu.SMEM)
    anywhere = pl.BlockSpec(memory_space=pl.ANY)
    whole = (CHUNKS, 4, 4, ROWS, WIDTH)
    units = [pltpu.VMEM((4, 4, ROWS, columns_of(n)[1]), jnp.bfloat16) for n in range(UNITS)]
    small = (4, 4, 8, 128)
    out, _ = pl.pallas_call(
        kernel,
        out_shape=(jax.ShapeDtypeStruct((16, 128), jnp.float32), jax.ShapeDtypeStruct(whole, jnp.bfloat16)),
        in_specs=[smem, anywhere, anywhere, anywhere],
        out_specs=(vmem, anywhere),
        scratch_shapes=[
            *units,
            *units,
            pltpu.VMEM(whole, jnp.bfloat16),
            *[pltpu.VMEM((16, ROWS, WIDEST), jnp.bfloat16) for _ in range(STAGES)],
            pltpu.VMEM((16, 128), jnp.int32),
            pltpu.SMEM((16, 8, 16), jnp.int32),
            pltpu.VMEM((16, 8, 128), jnp.float32),
            *[pltpu.VMEM(small, jnp.float32) for _ in range(5)],
            *[pltpu.VMEM((CHUNKS, 8, TILE), jnp.float32) for _ in range(3)],
            pltpu.VMEM((CHUNKS - LATE, TILE, 128), jnp.float32),
            pltpu.VMEM((CHUNKS, (CHUNKS - LATE) * TILE, TILE), jnp.float32),
            pltpu.VMEM((2 * (CHUNKS - LATE) * TILE, 128), jnp.float32),
            pltpu.VMEM((8, TILE), jnp.float32),
            pltpu.VMEM((8, 8, TILE), jnp.float32),
            pltpu.VMEM((16, 8, TILE), jnp.float32),
            pltpu.VMEM((16, 8, TILE), jnp.float32),
            pltpu.SMEM((8, 16), jnp.int32),
            pltpu.SemaphoreType.DMA((4, FLYING + 1)),
            pltpu.SemaphoreType.DMA((UNITS + 1, 3)),
            pltpu.SemaphoreType.DMA((4, FLYING + 1)),
            pltpu.SemaphoreType.DMA((STAGES,)),
            pltpu.SemaphoreType.DMA((2,)),
            pltpu.SemaphoreType.DMA((4,)),
        ],
        compiler_params=pltpu.CompilerParams(
            collective_id=0, has_side_effects=True, vmem_limit_bytes=62 * 2**20
        ),
        cost_estimate=pl.CostEstimate(flops=2 * 36 * 256 * 256 * 4096, bytes_accessed=64 * 2**20, transcendentals=2048),
    )(block_owner, routing, embeddings.reshape(16, 128, WIDTH), row_cluster.reshape(16, 128))
    return out.reshape(-1)


def solution(mesh):
    placed = (P(("owner", "worker"), None), P(("owner", "worker")), P(("owner", "worker")), P())
    return jax.shard_map(
        shards, mesh=mesh, in_specs=placed, out_specs=P(("owner", "worker")), check_vma=False
    )
```

```python
import jax
import jax.numpy as jnp
from jax import lax
from jax.experimental import pallas as pl
from jax.experimental.pallas import tpu as pltpu
from jax.sharding import PartitionSpec as P

MESH = pl.DeviceIdType.MESH
CHUNKS = 8
PARTS = 7
UNITS = 4 * PARTS
ROWS = 16
WIDTH = 4096
WIDEST = 2048
STAGES = 4
CUTS = ((0, 512), (512, 1536), (2048, 2048), (0, 1792), (1792, 1024), (2816, 768), (3584, 512))
LEVELS = 4
TILE = 256
NEG = -3.0e38
FAR = -1.0e30
FLYING = 3
AXES = {"A": "zxy", "B": "xzy", "C": "yzx", "D": "yxz"}
Y_STEPS = ((2, 0), (2, 1), (1, 0), (3, 1), (1, 1), (3, 0), (0, 1))
O_STEPS = tuple((a, b) for a in range(4) for b in range(4) if (a, b) != (0, 0))
LATE = 5
LABELS = UNITS
SENT, FIRST, MID_SOURCE, MID_TARGET, PLACES, KEY, HOME = range(7)


def kind(unit):
    return "ABCD"[unit // PARTS]


def chunk_of_unit(unit):
    return 2 * (unit // PARTS) + (1 if unit % PARTS >= 3 else 0)


def columns_of(unit):
    return CUTS[unit % PARTS]


def plan():
    steps = []
    queue = {"z": [], "x": [], "y": []}
    flying = {"z": [], "x": [], "y": []}
    free_at = {"z": 0, "x": 0, "y": 0}

    def fill(axis, now):
        while queue[axis] and len(flying[axis]) < FLYING:
            unit, stage = queue[axis].pop(0)
            free_at[axis] = max(free_at[axis], now) + columns_of(unit)[1]
            flying[axis].append((free_at[axis], unit, stage))
            steps.append(("go", unit, stage))

    for sub in range(PARTS):
        for letter in range(3):
            queue[AXES["ABCD"[letter]][0]].append((PARTS * letter + sub, 0))
    for sub in range(PARTS):
        queue["y"].append((3 * PARTS + sub, 0))
    for _ in range(FLYING):
        for axis in "zxy":
            unit, stage = queue[axis].pop(0)
            free_at[axis] += columns_of(unit)[1]
            flying[axis].append((free_at[axis], unit, stage))
            steps.append(("go", unit, stage))
    steps.append(("ready",))
    while any(flying.values()):
        now, axis = min((flying[axis][0][0], "zxy".index(axis)) for axis in "zxy" if flying[axis])
        axis = "zxy"[axis]
        _, unit, stage = flying[axis].pop(0)
        steps.append(("wait", unit, stage))
        fill(axis, now)
        if stage == 2:
            steps.append(("arrived", unit))
            continue
        if stage == (1 if kind(unit) in "AB" else 0):
            steps.append(("middle", unit))
        following = AXES[kind(unit)][stage + 1]
        queue[following].append((unit, stage + 1))
        fill(following, now)
    return steps


STEPS = plan()
ARRIVALS = tuple(chunk_of_unit(step[1]) for step in STEPS if step[0] == "arrived" and step[1] % PARTS in (2, 6))


def kernel(owners, routing_far, emb, lab_far, out, r1, *scratch):
    sends = scratch[0:UNITS]
    mids = scratch[UNITS : 2 * UNITS]
    (
        members, stage0, stage1, stage2, stage3, lab, routing, lab_0, lab_a, lab_b, lab_c, lab_d, lab_e, label_rows, scale_rows, best_rows, lane_best, partial, rest,
        result, gathered, relayed, home, tab, send_sem, recv_sem, local_sem, stage_sem, table_sem, back_sem,
    ) = scratch[2 * UNITS :]
    owner = lax.axis_index("owner")
    worker = lax.axis_index("worker")
    mz, mx = owner // 4, owner % 4
    my, mc = worker // 2, worker % 2

    def turn(value, step, size):
        return lax.rem(value + step, size)

    def owner_of(dz, dx):
        return turn(mz, dz, 4) * 4 + turn(mx, dx, 4)

    def worker_of(dy, dc):
        return turn(my, dy, 4) * 2 + turn(mc, dc, 2)

    stages = (stage0, stage1, stage2, stage3)

    def fetch(n, at):
        first, width = columns_of(n)
        return pltpu.make_async_copy(
            emb.at[:, pl.ds(ROWS * chunk_of_unit(n), ROWS), pl.ds(first, width)],
            stages[at].at[:, :, pl.ds(0, width)],
            stage_sem.at[at],
        )

    steps = STEPS
    order = [step[1] for step in steps if step[0] == "go" and step[2] == 0]
    for at in range(STAGES):
        fetch(order[at], at).start()
    routing_copy = pltpu.make_async_copy(routing_far, routing, table_sem.at[0])
    routing_copy.start()
    lab_copy = pltpu.make_async_copy(lab_far, lab, table_sem.at[1])
    lab_copy.start()
    barrier = pltpu.get_barrier_semaphore()
    for dz, dx in O_STEPS:
        pl.semaphore_signal(barrier, inc=1, device_id=(owner_of(dz, dx), worker), device_id_type=MESH)
    for dy, dc in Y_STEPS:
        pl.semaphore_signal(barrier, inc=1, device_id=(owner, worker_of(dy, dc)), device_id_type=MESH)

    def remote(src, dst, send, recv, to):
        return pltpu.make_async_remote_copy(
            src_ref=src, dst_ref=dst, send_sem=send, recv_sem=recv, device_id=to, device_id_type=MESH
        )

    def hop(axis, src, dst, send, recv, local):
        copies = []
        if axis == "z":
            for d in (2, 1, 3):
                to = turn(mz, d, 4)
                copies.append(remote(src.at[to], dst.at[mz], send, recv, (to * 4 + mx, worker)))
            here = (src.at[mz], dst.at[mz])
        elif axis == "x":
            for d in (2, 1, 3):
                to = turn(mx, d, 4)
                copies.append(remote(src.at[:, to], dst.at[:, mx], send, recv, (mz * 4 + to, worker)))
            here = (src.at[:, mx], dst.at[:, mx])
        else:
            for dy, dc in Y_STEPS:
                to = worker_of(dy, dc)
                copies.append(
                    remote(src.at[to // 2, pl.ds(2 * lax.rem(to, 2), 2)], dst.at[my, pl.ds(2 * mc, 2)], send, recv, (owner, to))
                )
            here = (src.at[my, pl.ds(2 * mc, 2)], dst.at[my, pl.ds(2 * mc, 2)])
        copies.append(pltpu.make_async_copy(here[0], here[1], local))
        return copies

    flying = {}
    started = {"z": 0, "x": 0, "y": 0}

    def all_of(like, sem):
        pltpu.make_async_copy(like, like, sem).wait()

    def wait(n, stage):
        axis, local, place = flying.pop((n, stage))
        like = size_of(n, axis)
        all_of(like, recv_sem.at[n, stage])
        local.wait()

    def size_of(n, axis):
        blocks = 14 if axis == "y" else 12
        return lab_0.at[pl.ds(0, blocks)] if n == LABELS else stage0.at[pl.ds(0, blocks), :, pl.ds(0, columns_of(n)[1])]

    sending = {}

    def sent(place):
        if place in sending:
            n, axis = sending.pop(place)
            all_of(size_of(n, axis), send_sem.at[place])

    def permute(row, src, dst, flat=False, width=None):
        def body(slot, carry):
            index = tab[row, slot]
            if width is not None:
                dst[slot >> 2, slot & 3] = src[index, :, pl.ds(0, width)]
            elif flat:
                dst[slot >> 2, slot & 3] = src[index]
            else:
                dst[slot >> 2, slot & 3] = src[index >> 2, index & 3]
            return carry

        lax.fori_loop(0, 16, body, 0)

    def route(n):
        if n == LABELS:
            return "zxy", ((lab_a, lab_b), (lab_b, lab_c), (lab_d, lab_e))
        columns = pl.ds(*columns_of(n))
        s, r, m = sends[n], r1.at[chunk_of_unit(n), :, :, :, columns], mids[n]
        f = members.at[ARRIVALS.index(chunk_of_unit(n)), :, :, :, columns]
        return AXES[kind(n)], ((s, r), (r, m), (s, f)) if kind(n) in "AB" else ((s, m), (s, r), (r, f))

    def go(n, stage):
        axes, ends = route(n)
        axis = axes[stage]
        if n == LABELS:
            place = (3, stage)
        else:
            place = ("zxy".index(axis), started[axis] % (FLYING + 1))
            started[axis] += 1
        sent(place)
        sending[place] = (n, axis)
        copies = hop(axis, *ends[stage], send_sem.at[place], recv_sem.at[n, stage], local_sem.at[place])
        flying[n, stage] = (axis, copies[-1], place)
        for copy in copies:
            copy.start()

    def middle(n):
        for place in [place for place in sending if sending[place][0] == n]:
            sent(place)
        if n == LABELS:
            permute(MID_SOURCE, lab_c, lab_d)
        else:
            permute(MID_SOURCE if kind(n) in "AB" else MID_TARGET, mids[n], sends[n])

    def invert(row, keys, payload):
        def body(slot, carry):
            found = jnp.int32(0)
            for i in range(16):
                found += jnp.where(keys(i) == slot, payload(i), 0)
            tab[row, slot] = found & 15
            return carry

        lax.fori_loop(0, 16, body, 0)

    def ranked(row, values):
        def body(slot, carry):
            value = values(slot)
            count = jnp.int32(0)
            for i in range(16):
                count += jnp.where((values(i) == value) & (i < slot), 1, 0)
            tab[row, slot] = 2 * value + count
            return carry

        lax.fori_loop(0, 16, body, 0)

    def find(row, values):
        def body(slot, counts):
            found = jnp.int32(0)
            after = []
            for w in range(8):
                hit = values(slot, w) == worker
                found += jnp.where(hit, 2 * w + counts[w], 0)
                after.append(counts[w] + jnp.where(hit, 1, 0))
            tab[row, slot] = found & 15
            return tuple(after)

        lax.fori_loop(0, 16, body, tuple(jnp.int32(0) for _ in range(8)))

    def home_slots():
        def body(slot, carry):
            target = owners[slot]
            mine = routing[target, worker, owner]
            count = jnp.int32(0)
            for i in range(16):
                count += jnp.where((routing[target, worker, i] == mine) & (i < owner), 1, 0)
            tab[HOME, slot] = 2 * worker + count
            return carry

        lax.fori_loop(0, 16, body, 0)

    lane = lax.broadcasted_iota(jnp.int32, (1, TILE), 1)
    eye = lax.broadcasted_iota(jnp.int32, (TILE, TILE), 0) == lax.broadcasted_iota(jnp.int32, (TILE, TILE), 1)
    chunk_half = lax.broadcasted_iota(jnp.int32, (8, 128), 0)
    place_half = lax.broadcasted_iota(jnp.int32, (8, 128), 1) // 16
    on_place = place_half == chunk_half

    def spread(x):
        for shift in (64, 32, 16):
            x = x + pltpu.roll(x, shift, 1)
        return x

    def label_tiles():
        for block in range(16):
            row = lab[block : block + 1, :].astype(jnp.float32)
            lab_0[block] = spread(jnp.where(on_place, row, 0.0))

    invert(SENT, lambda i: owners[i], lambda i: i)
    prepared = []

    def prepare(n):
        at = len(prepared)
        prepared.append(n)
        fetch(n, at % STAGES).wait()
        permute(SENT if kind(n) in "AB" else FIRST, stages[at % STAGES], sends[n], width=columns_of(n)[1])
        if at + STAGES < UNITS:
            fetch(order[at + STAGES], at % STAGES).start()

    def as_column(row):
        column = jnp.transpose(jnp.broadcast_to(row, (128, TILE)))
        return jnp.concatenate([column, column], axis=1)

    def product(first, count, j, columns):
        a = members[first : first + count, :, :, :, columns].reshape(count * TILE, columns.stop - columns.start)
        b = members[j, :, :, :, columns].reshape(TILE, columns.stop - columns.start)
        return lax.dot_general(a, b, (((1,), (1,)), ((), ())), preferred_element_type=jnp.float32)

    whole = slice(0, WIDTH)
    late_count = CHUNKS - LATE

    def part(level):
        first, width = CUTS[3 + level]
        return slice(first, first + width)

    def wide(at):
        column = rest[at * TILE : (at + 1) * TILE]
        return jnp.concatenate([column, column], axis=1)

    def keep(x, labels, j):
        return jnp.where(labels == label_rows[j][0:1], x, FAR)

    def late_products(level):
        if level == 0:
            for at in range(late_count):
                rest[at * TILE : (at + 1) * TILE] = as_column(label_rows[LATE + at][0:1])[:, :128]

        def body(j, carry):
            total = product(LATE, late_count, j, part(level))
            for at in range(late_count):
                rows = slice(at * TILE, (at + 1) * TILE)
                if level == 0:
                    partial[j, rows] = keep(total[rows], wide(at), j)
                else:
                    partial[j, rows] = partial[j, rows] + total[rows]
            return carry

        lax.fori_loop(0, LATE, body, 0)
        for j in range(LATE, CHUNKS):
            total = product(j, CHUNKS - j, j, part(level))
            for i in range(j, CHUNKS):
                rows, own = slice((i - LATE) * TILE, (i - LATE + 1) * TILE), total[(i - j) * TILE : (i - j + 1) * TILE]
                if level > 0:
                    own = own + partial[j, rows]
                elif i > j:
                    own = keep(own, wide(i - LATE), j)
                partial[j, rows] = own

    def gram_labels(i):
        n = ARRIVALS[i]
        row = jnp.zeros((1, TILE), jnp.float32)
        for slot in range(16):
            if n < 4:
                tile = lab_e[slot // 4, slot % 4]
            else:
                index = tab[PLACES, slot]
                tile = lab_e[index >> 2, index & 3]
            piece = tile[n : n + 1, :]
            row = jnp.where(lane // 16 == slot, jnp.concatenate([piece, piece], axis=1), row)
        label_rows[i] = jnp.broadcast_to(row, (8, TILE))

    def own_scores(i, own):
        row = label_rows[i][0:1]
        labels = as_column(row)
        scale = lax.rsqrt(jnp.sum(jnp.where(eye, own, 0.0), axis=0, keepdims=True) / WIDTH + 1e-6)
        scale_rows[i] = jnp.broadcast_to(scale, (8, TILE))
        scales = as_column(scale)
        scored = jnp.where((labels == row) & jnp.logical_not(eye), own * scales, NEG)
        best_rows[i] = jnp.broadcast_to(jnp.max(scored, axis=0, keepdims=True), (8, TILE))
        return labels, scales

    def pair(other, scales, j):
        down = jnp.max(other * scales, axis=0, keepdims=True)
        best_rows[j] = jnp.maximum(best_rows[j], jnp.broadcast_to(down, (8, TILE)))
        across = other * scale_rows[j][0:1]
        return jnp.maximum(across[:, :128], across[:, 128:])

    def settle(i, at):
        turned = jnp.max(jnp.transpose(lane_best[at]), axis=0, keepdims=True)
        best_rows[i] = jnp.maximum(best_rows[i], jnp.broadcast_to(turned, (8, TILE)))

    def gram(i):
        labels, scales = own_scores(i, product(i, 1, i, whole))
        lane_best[0] = jnp.full((TILE, 128), NEG, jnp.float32)

        def body(j, carry):
            lane_best[0] = jnp.maximum(lane_best[0], pair(keep(product(i, 1, j, whole), labels, j), scales, j))
            return carry

        if i > 0:
            lax.fori_loop(0, i, body, 0)
            settle(i, 0)

    def late_gram():
        last = part(LEVELS - 1)
        scales = [None] * late_count
        for at in range(late_count):
            lane_best[at] = jnp.full((TILE, 128), NEG, jnp.float32)
        for j in range(LATE, CHUNKS):
            at = j - LATE
            total = partial[j, at * TILE :] + product(j, CHUNKS - j, j, last)
            _, scales[at] = own_scores(j, total[:TILE])
            rest[at * TILE : (at + 1) * TILE] = scales[at][:, :128]
            partial[j, at * TILE :] = total
        for j in range(LATE, CHUNKS):
            for i in range(j + 1, CHUNKS):
                at = i - LATE
                lane_best[at] = jnp.maximum(lane_best[at], pair(partial[j, at * TILE : (at + 1) * TILE], scales[at], j))

        def body(j, carry):
            total = partial[j] + product(LATE, late_count, j, last)
            for at in range(late_count):
                lane_best[at] = jnp.maximum(lane_best[at], pair(total[at * TILE : (at + 1) * TILE], wide(at), j))
            return carry

        lax.fori_loop(0, LATE, body, 0)
        for at in range(late_count):
            settle(LATE + at, at)

    greeted = []
    done = []
    arrived = set()
    for step in steps:
        if step[0] == "go":
            _, n, stage = step
            if stage == 0 and n not in prepared:
                if kind(n) in "CD" and not any(kind(m) in "CD" for m in prepared):
                    routing_copy.wait()
                    ranked(KEY, lambda i: routing[i, worker, owner])
                    invert(FIRST, lambda i: tab[KEY, i], lambda i: tab[SENT, i])
                prepare(n)
            if not greeted:
                greeted.append(True)
                pl.semaphore_wait(barrier, len(O_STEPS) + len(Y_STEPS))
            go(n, stage)
        elif step[0] == "ready":
            lab_copy.wait()
            label_tiles()
            permute(SENT, lab_0, lab_a, flat=True)
            go(LABELS, 0)
            ranked(KEY, lambda i: routing[owner, worker, i])
            invert(MID_SOURCE, lambda i: tab[KEY, i], lambda i: i)
            find(MID_TARGET, lambda i, w: routing[i, w, owner])
            find(PLACES, lambda i, w: routing[owner, w, i])
            home_slots()
            while len(prepared) < UNITS:
                prepare(order[len(prepared)])
        elif step[0] == "wait":
            _, n, stage = step
            wait(n, stage)
            if n == 1 and stage < 2:
                wait(LABELS, stage)
                if stage == 1:
                    middle(LABELS)
                go(LABELS, stage + 1)
        elif step[0] == "middle":
            middle(step[1])
        else:
            n = step[1]
            if not arrived:
                wait(LABELS, 2)
                for i in range(CHUNKS):
                    gram_labels(i)
            arrived.add(n)
            i = ARRIVALS.index(chunk_of_unit(n))
            if n % PARTS in (2, 6) and i < LATE:
                assert all(m in arrived for m in range(UNITS) if chunk_of_unit(m) in ARRIVALS[: i + 1]), "order"
                gram(i)
            while len(done) < LEVELS:
                level = len(done)
                after = {m for m in range(UNITS) if chunk_of_unit(m) in ARRIVALS[LATE:] and m % PARTS > 3 + level}
                if arrived | after != set(range(UNITS)):
                    break
                done.append(level)
                if level < LEVELS - 1:
                    late_products(level)
                else:
                    late_gram()
    assert len(done) == LEVELS, "order"

    for i, n in enumerate(ARRIVALS):
        result[n : n + 1, :] = best_rows[i][0:1] * scale_rows[i][0:1] / WIDTH
    for dy, dc in Y_STEPS:
        remote(result, gathered.at[worker], back_sem.at[0], back_sem.at[1], (owner, worker_of(dy, dc))).start()
    gathered[worker] = result[...]
    all_of(gathered.at[pl.ds(0, 7)], back_sem.at[1])
    for slot in range(16):
        relayed[slot] = gathered[routing[owner, worker, slot]]
    for dz, dx in O_STEPS:
        to = owner_of(dz, dx)
        remote(relayed.at[to], home.at[owner], back_sem.at[2], back_sem.at[3], (to, worker)).start()
    home[owner] = relayed[owner]
    all_of(home.at[pl.ds(0, 15)], back_sem.at[3])

    chunk = lax.broadcasted_iota(jnp.int32, (8, TILE), 0)
    place = lax.broadcasted_iota(jnp.int32, (8, TILE), 1) // 16
    kept = []
    for block in range(16):
        tile = home[owners[block]]
        tile = jnp.where(place == jnp.where(chunk < 4, tab[HOME, block], owner), tile, 0.0)
        kept.append(tile[:, :128] + tile[:, 128:])
    kept = spread(jnp.concatenate(kept, axis=0)).reshape(16, 8, 128)
    out[...] = jnp.sum(jnp.where(on_place, kept, 0.0), axis=1)
    all_of(gathered.at[pl.ds(0, 7)], back_sem.at[0])
    all_of(home.at[pl.ds(0, 15)], back_sem.at[2])
    for place in list(sending):
        sent(place)


def shards(embeddings, row_cluster, block_owner, routing):
    vmem = pl.BlockSpec(memory_space=pltpu.VMEM)
    smem = pl.BlockSpec(memory_space=pltpu.SMEM)
    anywhere = pl.BlockSpec(memory_space=pl.ANY)
    whole = (CHUNKS, 4, 4, ROWS, WIDTH)
    units = [pltpu.VMEM((4, 4, ROWS, columns_of(n)[1]), jnp.bfloat16) for n in range(UNITS)]
    small = (4, 4, 8, 128)
    out, _ = pl.pallas_call(
        kernel,
        out_shape=(jax.ShapeDtypeStruct((16, 128), jnp.float32), jax.ShapeDtypeStruct(whole, jnp.bfloat16)),
        in_specs=[smem, anywhere, anywhere, anywhere],
        out_specs=(vmem, anywhere),
        scratch_shapes=[
            *units,
            *units,
            pltpu.VMEM(whole, jnp.bfloat16),
            *[pltpu.VMEM((16, ROWS, WIDEST), jnp.bfloat16) for _ in range(STAGES)],
            pltpu.VMEM((16, 128), jnp.int32),
            pltpu.SMEM((16, 8, 16), jnp.int32),
            pltpu.VMEM((16, 8, 128), jnp.float32),
            *[pltpu.VMEM(small, jnp.float32) for _ in range(5)],
            *[pltpu.VMEM((CHUNKS, 8, TILE), jnp.float32) for _ in range(3)],
            pltpu.VMEM((CHUNKS - LATE, TILE, 128), jnp.float32),
            pltpu.VMEM((CHUNKS, (CHUNKS - LATE) * TILE, TILE), jnp.float32),
            pltpu.VMEM((2 * (CHUNKS - LATE) * TILE, 128), jnp.float32),
            pltpu.VMEM((8, TILE), jnp.float32),
            pltpu.VMEM((8, 8, TILE), jnp.float32),
            pltpu.VMEM((16, 8, TILE), jnp.float32),
            pltpu.VMEM((16, 8, TILE), jnp.float32),
            pltpu.SMEM((8, 16), jnp.int32),
            pltpu.SemaphoreType.DMA((4, FLYING + 1)),
            pltpu.SemaphoreType.DMA((UNITS + 1, 3)),
            pltpu.SemaphoreType.DMA((4, FLYING + 1)),
            pltpu.SemaphoreType.DMA((STAGES,)),
            pltpu.SemaphoreType.DMA((2,)),
            pltpu.SemaphoreType.DMA((4,)),
        ],
        compiler_params=pltpu.CompilerParams(
            collective_id=0, has_side_effects=True, vmem_limit_bytes=62 * 2**20
        ),
        cost_estimate=pl.CostEstimate(flops=2 * 36 * 256 * 256 * 4096, bytes_accessed=64 * 2**20, transcendentals=2048),
    )(block_owner, routing, embeddings.reshape(16, 128, WIDTH), row_cluster.reshape(16, 128))
    return jnp.maximum(out.reshape(-1), -1.0)


def solution(mesh):
    placed = (P(("owner", "worker"), None), P(("owner", "worker")), P(("owner", "worker")), P())
    return jax.shard_map(
        shards, mesh=mesh, in_specs=placed, out_specs=P(("owner", "worker")), check_vma=False
    )
```

```python
import jax
import jax.numpy as jnp
from jax import lax
from jax.experimental import pallas as pl
from jax.experimental.pallas import tpu as pltpu
from jax.sharding import PartitionSpec as P

MESH = pl.DeviceIdType.MESH
CHUNKS = 8
PARTS = 7
UNITS = 4 * PARTS
ROWS = 16
WIDTH = 4096
WIDEST = 2048
STAGES = 4
CUTS = ((0, 512), (512, 1536), (2048, 2048), (0, 1792), (1792, 1024), (2816, 768), (3584, 512))
LEVELS = 4
TILE = 256
NEG = -3.0e38
FAR = -1.0e30
FLYING = 3
AXES = {"A": "zxy", "B": "xzy", "C": "yzx", "D": "yxz"}
Y_STEPS = ((2, 0), (2, 1), (1, 0), (3, 1), (1, 1), (3, 0), (0, 1))
HOPS = (0, 1, 2, 1)
O_STEPS = tuple(
    sorted(((a, b) for a in range(4) for b in range(4) if (a, b) != (0, 0)), key=lambda step: -HOPS[step[0]] - HOPS[step[1]])
)
LATE = 5
LABELS = UNITS
SENT, FIRST, MID_SOURCE, MID_TARGET, PLACES, KEY, HOME = range(7)


def kind(unit):
    return "ABCD"[unit // PARTS]


def chunk_of_unit(unit):
    return 2 * (unit // PARTS) + (1 if unit % PARTS >= 3 else 0)


def columns_of(unit):
    return CUTS[unit % PARTS]


def plan():
    steps = []
    queue = {"z": [], "x": [], "y": []}
    flying = {"z": [], "x": [], "y": []}
    free_at = {"z": 0, "x": 0, "y": 0}

    def fill(axis, now):
        while queue[axis] and len(flying[axis]) < FLYING:
            unit, stage = queue[axis].pop(0)
            free_at[axis] = max(free_at[axis], now) + columns_of(unit)[1]
            flying[axis].append((free_at[axis], unit, stage))
            steps.append(("go", unit, stage))

    for sub in range(PARTS):
        for letter in range(3):
            queue[AXES["ABCD"[letter]][0]].append((PARTS * letter + sub, 0))
    for sub in range(PARTS):
        queue["y"].append((3 * PARTS + sub, 0))
    for _ in range(FLYING):
        for axis in "zxy":
            unit, stage = queue[axis].pop(0)
            free_at[axis] += columns_of(unit)[1]
            flying[axis].append((free_at[axis], unit, stage))
            steps.append(("go", unit, stage))
    steps.append(("ready",))
    while any(flying.values()):
        now, axis = min((flying[axis][0][0], "zxy".index(axis)) for axis in "zxy" if flying[axis])
        axis = "zxy"[axis]
        _, unit, stage = flying[axis].pop(0)
        steps.append(("wait", unit, stage))
        fill(axis, now)
        if stage == 2:
            steps.append(("arrived", unit))
            continue
        if stage == (1 if kind(unit) in "AB" else 0):
            steps.append(("middle", unit))
        following = AXES[kind(unit)][stage + 1]
        queue[following].append((unit, stage + 1))
        fill(following, now)
    return steps


STEPS = plan()
ARRIVALS = tuple(chunk_of_unit(step[1]) for step in STEPS if step[0] == "arrived" and step[1] % PARTS in (2, 6))


def kernel(owners, routing_far, emb, lab_far, out, r1, *scratch):
    sends = scratch[0:UNITS]
    mids = scratch[UNITS : 2 * UNITS]
    (
        members, stage0, stage1, stage2, stage3, lab, routing, lab_0, lab_a, lab_b, lab_c, lab_d, lab_e, label_rows, scale_rows, best_rows, lane_best, partial, rest,
        result, gathered, relayed, home, tab, send_sem, recv_sem, local_sem, stage_sem, table_sem, back_sem,
    ) = scratch[2 * UNITS :]
    owner = lax.axis_index("owner")
    worker = lax.axis_index("worker")
    mz, mx = owner // 4, owner % 4
    my, mc = worker // 2, worker % 2

    def turn(value, step, size):
        return lax.rem(value + step, size)

    def owner_of(dz, dx):
        return turn(mz, dz, 4) * 4 + turn(mx, dx, 4)

    def worker_of(dy, dc):
        return turn(my, dy, 4) * 2 + turn(mc, dc, 2)

    stages = (stage0, stage1, stage2, stage3)

    def fetch(n, at):
        first, width = columns_of(n)
        return pltpu.make_async_copy(
            emb.at[:, pl.ds(ROWS * chunk_of_unit(n), ROWS), pl.ds(first, width)],
            stages[at].at[:, :, pl.ds(0, width)],
            stage_sem.at[at],
        )

    steps = STEPS
    order = [step[1] for step in steps if step[0] == "go" and step[2] == 0]
    for at in range(STAGES):
        fetch(order[at], at).start()
    routing_copy = pltpu.make_async_copy(routing_far, routing, table_sem.at[0])
    routing_copy.start()
    lab_copy = pltpu.make_async_copy(lab_far, lab, table_sem.at[1])
    lab_copy.start()
    barrier = pltpu.get_barrier_semaphore()
    for dz, dx in O_STEPS:
        pl.semaphore_signal(barrier, inc=1, device_id=(owner_of(dz, dx), worker), device_id_type=MESH)
    for dy, dc in Y_STEPS:
        pl.semaphore_signal(barrier, inc=1, device_id=(owner, worker_of(dy, dc)), device_id_type=MESH)

    def remote(src, dst, send, recv, to):
        return pltpu.make_async_remote_copy(
            src_ref=src, dst_ref=dst, send_sem=send, recv_sem=recv, device_id=to, device_id_type=MESH
        )

    def hop(axis, src, dst, send, recv, local):
        copies = []
        if axis == "z":
            for d in (2, 1, 3):
                to = turn(mz, d, 4)
                copies.append(remote(src.at[to], dst.at[mz], send, recv, (to * 4 + mx, worker)))
            here = (src.at[mz], dst.at[mz])
        elif axis == "x":
            for d in (2, 1, 3):
                to = turn(mx, d, 4)
                copies.append(remote(src.at[:, to], dst.at[:, mx], send, recv, (mz * 4 + to, worker)))
            here = (src.at[:, mx], dst.at[:, mx])
        else:
            for dy, dc in Y_STEPS:
                to = worker_of(dy, dc)
                copies.append(
                    remote(src.at[to // 2, pl.ds(2 * lax.rem(to, 2), 2)], dst.at[my, pl.ds(2 * mc, 2)], send, recv, (owner, to))
                )
            here = (src.at[my, pl.ds(2 * mc, 2)], dst.at[my, pl.ds(2 * mc, 2)])
        copies.append(pltpu.make_async_copy(here[0], here[1], local))
        return copies

    flying = {}
    started = {"z": 0, "x": 0, "y": 0}

    def all_of(like, sem):
        pltpu.make_async_copy(like, like, sem).wait()

    def wait(n, stage):
        axis, local, place = flying.pop((n, stage))
        like = size_of(n, axis)
        all_of(like, recv_sem.at[n, stage])
        local.wait()

    def size_of(n, axis):
        blocks = 14 if axis == "y" else 12
        return lab_0.at[pl.ds(0, blocks)] if n == LABELS else stage0.at[pl.ds(0, blocks), :, pl.ds(0, columns_of(n)[1])]

    sending = {}

    def sent(place):
        if place in sending:
            n, axis = sending.pop(place)
            all_of(size_of(n, axis), send_sem.at[place])

    def permute(row, src, dst, flat=False, width=None):
        def body(slot, carry):
            index = tab[row, slot]
            if width is not None:
                dst[slot >> 2, slot & 3] = src[index, :, pl.ds(0, width)]
            elif flat:
                dst[slot >> 2, slot & 3] = src[index]
            else:
                dst[slot >> 2, slot & 3] = src[index >> 2, index & 3]
            return carry

        lax.fori_loop(0, 16, body, 0)

    def route(n):
        if n == LABELS:
            return "zxy", ((lab_a, lab_b), (lab_b, lab_c), (lab_d, lab_e))
        columns = pl.ds(*columns_of(n))
        s, r, m = sends[n], r1.at[chunk_of_unit(n), :, :, :, columns], mids[n]
        f = members.at[ARRIVALS.index(chunk_of_unit(n)), :, :, :, columns]
        return AXES[kind(n)], ((s, r), (r, m), (s, f)) if kind(n) in "AB" else ((s, m), (s, r), (r, f))

    def go(n, stage):
        axes, ends = route(n)
        axis = axes[stage]
        if n == LABELS:
            place = (3, stage)
        else:
            place = ("zxy".index(axis), started[axis] % (FLYING + 1))
            started[axis] += 1
        sent(place)
        sending[place] = (n, axis)
        copies = hop(axis, *ends[stage], send_sem.at[place], recv_sem.at[n, stage], local_sem.at[place])
        flying[n, stage] = (axis, copies[-1], place)
        for copy in copies:
            copy.start()

    def middle(n):
        for place in [place for place in sending if sending[place][0] == n]:
            sent(place)
        if n == LABELS:
            permute(MID_SOURCE, lab_c, lab_d)
        else:
            permute(MID_SOURCE if kind(n) in "AB" else MID_TARGET, mids[n], sends[n])

    def invert(row, keys, payload):
        def body(slot, carry):
            found = jnp.int32(0)
            for i in range(16):
                found += jnp.where(keys(i) == slot, payload(i), 0)
            tab[row, slot] = found & 15
            return carry

        lax.fori_loop(0, 16, body, 0)

    def ranked(row, values):
        def body(slot, carry):
            value = values(slot)
            count = jnp.int32(0)
            for i in range(16):
                count += jnp.where((values(i) == value) & (i < slot), 1, 0)
            tab[row, slot] = 2 * value + count
            return carry

        lax.fori_loop(0, 16, body, 0)

    def find(row, values):
        def body(slot, counts):
            found = jnp.int32(0)
            after = []
            for w in range(8):
                hit = values(slot, w) == worker
                found += jnp.where(hit, 2 * w + counts[w], 0)
                after.append(counts[w] + jnp.where(hit, 1, 0))
            tab[row, slot] = found & 15
            return tuple(after)

        lax.fori_loop(0, 16, body, tuple(jnp.int32(0) for _ in range(8)))

    def home_slots():
        def body(slot, carry):
            target = owners[slot]
            mine = routing[target, worker, owner]
            count = jnp.int32(0)
            for i in range(16):
                count += jnp.where((routing[target, worker, i] == mine) & (i < owner), 1, 0)
            tab[HOME, slot] = 2 * worker + count
            return carry

        lax.fori_loop(0, 16, body, 0)

    lane = lax.broadcasted_iota(jnp.int32, (1, TILE), 1)
    eye = lax.broadcasted_iota(jnp.int32, (TILE, TILE), 0) == lax.broadcasted_iota(jnp.int32, (TILE, TILE), 1)
    chunk_half = lax.broadcasted_iota(jnp.int32, (8, 128), 0)
    place_half = lax.broadcasted_iota(jnp.int32, (8, 128), 1) // 16
    on_place = place_half == chunk_half

    def spread(x):
        for shift in (64, 32, 16):
            x = x + pltpu.roll(x, shift, 1)
        return x

    def label_tiles():
        for block in range(16):
            row = lab[block : block + 1, :].astype(jnp.float32)
            lab_0[block] = spread(jnp.where(on_place, row, 0.0))

    invert(SENT, lambda i: owners[i], lambda i: i)
    prepared = []

    def prepare(n):
        at = len(prepared)
        prepared.append(n)
        fetch(n, at % STAGES).wait()
        permute(SENT if kind(n) in "AB" else FIRST, stages[at % STAGES], sends[n], width=columns_of(n)[1])
        if at + STAGES < UNITS:
            fetch(order[at + STAGES], at % STAGES).start()

    def as_column(row):
        column = jnp.transpose(jnp.broadcast_to(row, (128, TILE)))
        return jnp.concatenate([column, column], axis=1)

    def product(first, count, j, columns):
        a = members[first : first + count, :, :, :, columns].reshape(count * TILE, columns.stop - columns.start)
        b = members[j, :, :, :, columns].reshape(TILE, columns.stop - columns.start)
        return lax.dot_general(a, b, (((1,), (1,)), ((), ())), preferred_element_type=jnp.float32)

    whole = slice(0, WIDTH)
    late_count = CHUNKS - LATE

    def part(level):
        first, width = CUTS[3 + level]
        return slice(first, first + width)

    def wide(at):
        column = rest[at * TILE : (at + 1) * TILE]
        return jnp.concatenate([column, column], axis=1)

    def keep(x, labels, j):
        return jnp.where(labels == label_rows[j][0:1], x, FAR)

    def late_products(level):
        if level == 0:
            for at in range(late_count):
                rest[at * TILE : (at + 1) * TILE] = as_column(label_rows[LATE + at][0:1])[:, :128]

        def body(j, carry):
            total = product(LATE, late_count, j, part(level))
            for at in range(late_count):
                rows = slice(at * TILE, (at + 1) * TILE)
                if level == 0:
                    partial[j, rows] = keep(total[rows], wide(at), j)
                else:
                    partial[j, rows] = partial[j, rows] + total[rows]
            return carry

        lax.fori_loop(0, LATE, body, 0)
        for j in range(LATE, CHUNKS):
            total = product(j, CHUNKS - j, j, part(level))
            for i in range(j, CHUNKS):
                rows, own = slice((i - LATE) * TILE, (i - LATE + 1) * TILE), total[(i - j) * TILE : (i - j + 1) * TILE]
                if level > 0:
                    own = own + partial[j, rows]
                elif i > j:
                    own = keep(own, wide(i - LATE), j)
                partial[j, rows] = own

    def gram_labels(i):
        n = ARRIVALS[i]
        row = jnp.zeros((1, TILE), jnp.float32)
        for slot in range(16):
            if n < 4:
                tile = lab_e[slot // 4, slot % 4]
            else:
                index = tab[PLACES, slot]
                tile = lab_e[index >> 2, index & 3]
            piece = tile[n : n + 1, :]
            row = jnp.where(lane // 16 == slot, jnp.concatenate([piece, piece], axis=1), row)
        label_rows[i] = jnp.broadcast_to(row, (8, TILE))

    def own_scores(i, own):
        row = label_rows[i][0:1]
        labels = as_column(row)
        scale = lax.rsqrt(jnp.sum(jnp.where(eye, own, 0.0), axis=0, keepdims=True) / WIDTH + 1e-6)
        scale_rows[i] = jnp.broadcast_to(scale, (8, TILE))
        scales = as_column(scale)
        scored = jnp.where((labels == row) & jnp.logical_not(eye), own * scales, NEG)
        best_rows[i] = jnp.broadcast_to(jnp.max(scored, axis=0, keepdims=True), (8, TILE))
        return labels, scales

    def pair(other, scales, j):
        down = jnp.max(other * scales, axis=0, keepdims=True)
        best_rows[j] = jnp.maximum(best_rows[j], jnp.broadcast_to(down, (8, TILE)))
        across = other * scale_rows[j][0:1]
        return jnp.maximum(across[:, :128], across[:, 128:])

    def settle(i, at):
        turned = jnp.max(jnp.transpose(lane_best[at]), axis=0, keepdims=True)
        best_rows[i] = jnp.maximum(best_rows[i], jnp.broadcast_to(turned, (8, TILE)))

    def gram(i):
        labels, scales = own_scores(i, product(i, 1, i, whole))
        lane_best[0] = jnp.full((TILE, 128), NEG, jnp.float32)

        def body(j, carry):
            lane_best[0] = jnp.maximum(lane_best[0], pair(keep(product(i, 1, j, whole), labels, j), scales, j))
            return carry

        if i > 0:
            lax.fori_loop(0, i, body, 0)
            settle(i, 0)

    def late_gram():
        last = part(LEVELS - 1)
        scales = [None] * late_count
        for at in range(late_count):
            lane_best[at] = jnp.full((TILE, 128), NEG, jnp.float32)
        for j in range(LATE, CHUNKS):
            at = j - LATE
            total = partial[j, at * TILE :] + product(j, CHUNKS - j, j, last)
            _, scales[at] = own_scores(j, total[:TILE])
            rest[at * TILE : (at + 1) * TILE] = scales[at][:, :128]
            partial[j, at * TILE :] = total
        for j in range(LATE, CHUNKS):
            for i in range(j + 1, CHUNKS):
                at = i - LATE
                lane_best[at] = jnp.maximum(lane_best[at], pair(partial[j, at * TILE : (at + 1) * TILE], scales[at], j))

        def body(j, carry):
            total = partial[j] + product(LATE, late_count, j, last)
            for at in range(late_count):
                lane_best[at] = jnp.maximum(lane_best[at], pair(total[at * TILE : (at + 1) * TILE], wide(at), j))
            return carry

        lax.fori_loop(0, LATE, body, 0)
        for at in range(late_count):
            settle(LATE + at, at)

    greeted = []
    done = []
    arrived = set()
    for step in steps:
        if step[0] == "go":
            _, n, stage = step
            if stage == 0 and n not in prepared:
                if kind(n) in "CD" and not any(kind(m) in "CD" for m in prepared):
                    routing_copy.wait()
                    ranked(KEY, lambda i: routing[i, worker, owner])
                    invert(FIRST, lambda i: tab[KEY, i], lambda i: tab[SENT, i])
                prepare(n)
            if not greeted:
                greeted.append(True)
                pl.semaphore_wait(barrier, len(O_STEPS) + len(Y_STEPS))
            go(n, stage)
        elif step[0] == "ready":
            lab_copy.wait()
            label_tiles()
            permute(SENT, lab_0, lab_a, flat=True)
            go(LABELS, 0)
            ranked(KEY, lambda i: routing[owner, worker, i])
            invert(MID_SOURCE, lambda i: tab[KEY, i], lambda i: i)
            find(MID_TARGET, lambda i, w: routing[i, w, owner])
            find(PLACES, lambda i, w: routing[owner, w, i])
            home_slots()
            while len(prepared) < UNITS:
                prepare(order[len(prepared)])
        elif step[0] == "wait":
            _, n, stage = step
            wait(n, stage)
            if n == 1 and stage < 2:
                wait(LABELS, stage)
                if stage == 1:
                    middle(LABELS)
                go(LABELS, stage + 1)
        elif step[0] == "middle":
            middle(step[1])
        else:
            n = step[1]
            if not arrived:
                wait(LABELS, 2)
                for i in range(CHUNKS):
                    gram_labels(i)
            arrived.add(n)
            i = ARRIVALS.index(chunk_of_unit(n))
            if n % PARTS in (2, 6) and i < LATE:
                assert all(m in arrived for m in range(UNITS) if chunk_of_unit(m) in ARRIVALS[: i + 1]), "order"
                gram(i)
            while len(done) < LEVELS:
                level = len(done)
                after = {m for m in range(UNITS) if chunk_of_unit(m) in ARRIVALS[LATE:] and m % PARTS > 3 + level}
                if arrived | after != set(range(UNITS)):
                    break
                done.append(level)
                if level < LEVELS - 1:
                    late_products(level)
                else:
                    late_gram()
    assert len(done) == LEVELS, "order"

    for i, n in enumerate(ARRIVALS):
        result[n : n + 1, :] = best_rows[i][0:1] * scale_rows[i][0:1] / WIDTH
    for dy, dc in Y_STEPS:
        remote(result, gathered.at[worker], back_sem.at[0], back_sem.at[1], (owner, worker_of(dy, dc))).start()
    gathered[worker] = result[...]
    all_of(gathered.at[pl.ds(0, 7)], back_sem.at[1])
    for slot in range(16):
        relayed[slot] = gathered[routing[owner, worker, slot]]
    for dz, dx in O_STEPS:
        to = owner_of(dz, dx)
        remote(relayed.at[to], home.at[owner], back_sem.at[2], back_sem.at[3], (to, worker)).start()
    home[owner] = relayed[owner]
    all_of(home.at[pl.ds(0, 15)], back_sem.at[3])

    chunk = lax.broadcasted_iota(jnp.int32, (8, TILE), 0)
    place = lax.broadcasted_iota(jnp.int32, (8, TILE), 1) // 16
    kept = []
    for block in range(16):
        tile = home[owners[block]]
        tile = jnp.where(place == jnp.where(chunk < 4, tab[HOME, block], owner), tile, 0.0)
        kept.append(tile[:, :128] + tile[:, 128:])
    kept = spread(jnp.concatenate(kept, axis=0)).reshape(16, 8, 128)
    out[...] = jnp.sum(jnp.where(on_place, kept, 0.0), axis=1)
    all_of(gathered.at[pl.ds(0, 7)], back_sem.at[0])
    all_of(home.at[pl.ds(0, 15)], back_sem.at[2])
    for place in list(sending):
        sent(place)


def shards(embeddings, row_cluster, block_owner, routing):
    vmem = pl.BlockSpec(memory_space=pltpu.VMEM)
    smem = pl.BlockSpec(memory_space=pltpu.SMEM)
    anywhere = pl.BlockSpec(memory_space=pl.ANY)
    whole = (CHUNKS, 4, 4, ROWS, WIDTH)
    units = [pltpu.VMEM((4, 4, ROWS, columns_of(n)[1]), jnp.bfloat16) for n in range(UNITS)]
    small = (4, 4, 8, 128)
    out, _ = pl.pallas_call(
        kernel,
        out_shape=(jax.ShapeDtypeStruct((16, 128), jnp.float32), jax.ShapeDtypeStruct(whole, jnp.bfloat16)),
        in_specs=[smem, anywhere, anywhere, anywhere],
        out_specs=(vmem, anywhere),
        scratch_shapes=[
            *units,
            *units,
            pltpu.VMEM(whole, jnp.bfloat16),
            *[pltpu.VMEM((16, ROWS, WIDEST), jnp.bfloat16) for _ in range(STAGES)],
            pltpu.VMEM((16, 128), jnp.int32),
            pltpu.SMEM((16, 8, 16), jnp.int32),
            pltpu.VMEM((16, 8, 128), jnp.float32),
            *[pltpu.VMEM(small, jnp.float32) for _ in range(5)],
            *[pltpu.VMEM((CHUNKS, 8, TILE), jnp.float32) for _ in range(3)],
            pltpu.VMEM((CHUNKS - LATE, TILE, 128), jnp.float32),
            pltpu.VMEM((CHUNKS, (CHUNKS - LATE) * TILE, TILE), jnp.float32),
            pltpu.VMEM((2 * (CHUNKS - LATE) * TILE, 128), jnp.float32),
            pltpu.VMEM((8, TILE), jnp.float32),
            pltpu.VMEM((8, 8, TILE), jnp.float32),
            pltpu.VMEM((16, 8, TILE), jnp.float32),
            pltpu.VMEM((16, 8, TILE), jnp.float32),
            pltpu.SMEM((8, 16), jnp.int32),
            pltpu.SemaphoreType.DMA((4, FLYING + 1)),
            pltpu.SemaphoreType.DMA((UNITS + 1, 3)),
            pltpu.SemaphoreType.DMA((4, FLYING + 1)),
            pltpu.SemaphoreType.DMA((STAGES,)),
            pltpu.SemaphoreType.DMA((2,)),
            pltpu.SemaphoreType.DMA((4,)),
        ],
        compiler_params=pltpu.CompilerParams(
            collective_id=0, has_side_effects=True, vmem_limit_bytes=62 * 2**20
        ),
        cost_estimate=pl.CostEstimate(flops=2 * 36 * 256 * 256 * 4096, bytes_accessed=64 * 2**20, transcendentals=2048),
    )(block_owner, routing, embeddings.reshape(16, 128, WIDTH), row_cluster.reshape(16, 128))
    return jnp.maximum(out.reshape(-1), -1.0)


def solution(mesh):
    placed = (P(("owner", "worker"), None), P(("owner", "worker")), P(("owner", "worker")), P())
    return jax.shard_map(
        shards, mesh=mesh, in_specs=placed, out_specs=P(("owner", "worker")), check_vma=False
    )
```
